32 devices in a mesh: groups: 1, grid: 32 (over z, y, x, core).
Axes of the slice: x: 2, y: 2, z: 4, core: 2. Of those that a mesh axis runs over, the one named last changes fastest.
Arguments:
- collocation: bfloat16 [512, 512, 512], P(('groups', 'grid')), may hold values from -0.25 to 0.25
- coords: float32 [512, 3, 512], P(('groups', 'grid')), may hold values from -6 to 6
- weights: float32 [512, 512], P(('groups', 'grid')), may hold values from 0.05 to 0.5
- owners: int32 [512, 16], P(('groups', 'grid')), may hold values from 0 to 31, all different within a row; in each aligned block of 16 rows (0 to 15, 16 to 31, ...) at most 8 rows name the same one
- slots: int32 [512, 16], P(('groups', 'grid')), may hold values from 0 to 31
- counts: int32 [512], P(('groups', 'grid')), may hold values from 2 to 4
- dens_tiles: bfloat16 [1024, 128, 128], P(('groups', 'grid')), may hold values from -6 to 6
- dens_scales: float32 [1024], P(('groups', 'grid')), may hold values from 0.5 to 2
- fock_prev: bfloat16 [1024, 128, 128], P(('groups', 'grid')), may hold values from -6 to 6
Outputs:
- fock: float32 [1024, 128, 128], P(('groups', 'grid'))
The draws below stay inside these ranges and needn't reach their ends.
Inputs may be any that keep to these rules, and one draw needn't show every extreme that they name: Each batch names 16 different owners; the batches of one device name one owner at most 8 times, a bound that some block reaches.
All inputs are finite; a program needn't handle non-finite values.
Results may differ from the reference program's by a relative error of at most 0.004.
Values may be sent and summed in bfloat16 or wider, within the bound.
A program may use at most 128 MiB of HBM per device.

```python
import math
import jax
import jax.numpy as jnp
import numpy as np
from jax import lax

TT = 128
L = 4
GB = 512
BPD = 16
TPD = 32
LF = 512
BATCHES = 512
TILES = 1024
MOST = 8


def draw_counts(key, part):
    key = jax.random.fold_in(key, 7)
    values = jax.random.randint(key, (BATCHES,), L // 2, L + 1)
    values = values.at[0].set(L).at[1].set(L // 2)
    return values.astype(jnp.int32)


def set_ends(entries, own_key, low, largest):
    longest = entries.shape.index(max(entries.shape))
    spots = []
    for shift in (0, 1):
        where = [jax.random.randint(jax.random.fold_in(own_key, axis), (), 0, length) for axis, length in enumerate(entries.shape)]
        where[longest] = (where[longest] + shift) % entries.shape[longest]
        spots.append(tuple(where))
    return entries.at[spots[0]].set(low).at[spots[1]].set(largest)


def block_levels(key, dims, pieces, smallest, top_value):
    def one(position, blocks):
        steps = jax.random.uniform(jax.random.fold_in(jax.random.fold_in(key, 6), position), (blocks,), jnp.float32, smallest / len(pieces), top_value / len(pieces))
        return jnp.repeat(jnp.exp(steps), dims[position] // blocks).reshape((-1,) + (1,) * (len(dims) - position - 1))

    gain = one(*pieces[0])
    for cut in pieces[1:]:
        gain = gain * one(*cut)
    return gain


def routed_block(rng, own, number, rows, number_of, top, limit, lean):
    sequence = jax.random.permutation(rng, number_of)
    packed, usual = portions_of(number_of, rows * top, limit, lean, True), portions_of(number_of, rows * top, limit, lean, False)
    places = jnp.arange(number_of)

    def named(lengths, rotation):
        used = int((lengths > 0).sum())
        fixed = max(1, used // 4)
        passed = fixed + (places - fixed + rotation * (used - fixed)) % max(1, number_of - fixed)
        return jnp.zeros((number_of,), jnp.int32).at[sequence[jnp.where(places < fixed, places, passed)]].set(jnp.asarray(lengths, jnp.int32))

    lengths = jnp.where(number % 4 == 0, named(packed, number // 4), named(usual, number - number // 4 - 1))
    mixed = jax.random.permutation(jax.random.fold_in(own, 3), number_of)
    giver, sink = mixed[0:number_of // 2 * 2:2], mixed[1:number_of // 2 * 2:2]
    slack = jnp.minimum(lengths[giver] - 1, limit - lengths[sink]) // 2
    slack = jnp.where((giver == sequence[0]) | (sink == sequence[0]) | (lengths[sink] == 0), 0, jnp.maximum(slack, 0))
    passed = jax.random.randint(jax.random.fold_in(own, 4), (number_of // 2,), 0, 1 << 20) % (slack + 1)
    lengths = lengths.at[giver].add(-passed).at[sink].add(passed)
    members = jnp.searchsorted(jnp.cumsum(lengths), jnp.arange(rows * top), side="right").astype(jnp.int32)
    listing = members.reshape(top, rows).T
    listing = listing[jax.random.permutation(jax.random.fold_in(own, 1), rows)]
    rotation = jax.random.randint(jax.random.fold_in(own, 2), (rows, 1), 0, top)
    return jnp.take_along_axis(listing, (jnp.arange(top)[None, :] + rotation) % top, axis=1)


def portions_of(count, total, most, skew, full):
    portions = [(1 << 20) // math.isqrt(grade ** skew) + 1 for grade in range(1, count + 1)]
    largest = most if full else min(most, max(-(-total // count), total * portions[0] // sum(portions)))
    least = 1 if total - largest >= count - 1 else 0
    given, spare = [largest] + [least] * (count - 1), total - largest - least * (count - 1)
    while spare > 0:
        free = [i for i in range(1, count) if given[i] < largest] or [i for i in range(1, count) if given[i] < most]
        mass, left = sum([portions[i] for i in free]), spare
        for i in free:
            addition = min(most - given[i], max(1, left * portions[i] // mass), spare)
            given[i] = given[i] + addition
            spare = spare - addition
    return np.array(given)


def gaussian(stream_key, extent, scale, limit, pieces=(), kind=jnp.bfloat16):
    factor_of = block_levels(stream_key, extent, pieces, -0.22, 0.18) if pieces else 1.0
    values = jax.random.normal(stream_key, extent, jnp.float32) * scale * factor_of
    return jnp.minimum(jnp.maximum(values, -limit), limit).astype(kind)


def setup_inputs(seed: int = 0, part: int = 0) -> dict:
    key_of = jax.random.split(jax.random.key(seed), 10)
    part_keys = jax.random.split(jax.random.fold_in(key_of[9], part), 10)
    collocation = gaussian(part_keys[0], (BATCHES, GB, LF), LF ** -0.5, 0.25, ((0, 32),))
    coords = gaussian(part_keys[1], (BATCHES, 3, GB), 1.5, 6.0, ((0, 32),), jnp.float32)
    weights = jnp.clip(jnp.exp(math.log(0.5) - 2.3025851 * jax.random.uniform(part_keys[2], (BATCHES, GB), jnp.float32) ** block_levels(part_keys[2], (BATCHES, GB), ((0, 32),), -0.2, 0.2)), 0.05, 0.5)
    owners_keys = jax.random.split(jax.random.fold_in(part_keys[3], 1), BATCHES // BPD)
    owners_turns = jax.random.permutation(jax.random.fold_in(part_keys[3], 3), BATCHES // BPD)
    owners = jax.vmap(lambda own, number: routed_block(jax.random.fold_in(part_keys[3], 2), own, number, BPD, BATCHES // BPD, L * L, MOST, 2))(owners_keys, owners_turns).reshape((BATCHES, L * L))
    slots = set_ends(jax.random.randint(part_keys[4], (BATCHES, L * L), 0, TPD), jax.random.fold_in(part_keys[4], 1), 0, TPD - 1).astype(jnp.int32)
    counts = draw_counts(jax.random.fold_in(jax.random.fold_in(key_of[9], part), 71), part)
    dens_tiles = gaussian(part_keys[6], (TILES, TT, TT), 1.0, 6.0, ((0, 32),))
    dens_scales = jnp.clip(jnp.exp(math.log(2.0) - 1.3862944 * jax.random.uniform(part_keys[7], (TILES,), jnp.float32) ** block_levels(part_keys[7], (TILES,), ((0, 32),), -0.2, 0.2)), 0.5, 2.0)
    fock_prev = gaussian(part_keys[8], (TILES, TT, TT), 1.0, 6.0, ((0, 32),))
    return {"collocation": collocation, "coords": coords, "weights": weights, "owners": owners, "slots": slots, "counts": counts, "dens_tiles": dens_tiles, "dens_scales": dens_scales, "fock_prev": fock_prev}


SOFTEN = 0.5

def reference(collocation, coords, weights, owners, slots, counts, dens_tiles, dens_scales, fock_prev):

    def batch_term(pool, input_arrays):
        collocation_matrix, tile_placement, quadrature_weight, owning_row, slot_index_row, tile_count = input_arrays
        index = (owning_row * TPD + slot_index_row).astype(jnp.int32)
        live = jnp.arange(L) < tile_count
        live_pair = (live[:, None] & live[None, :]).reshape(L * L)
        tiles = dens_tiles[index].astype(jnp.float32) * dens_scales[index][:, None, None]
        blocks = jnp.where(live_pair[:, None, None], tiles, 0.0).astype(jnp.bfloat16)
        density_delta = blocks.reshape(L, L, TT, TT).transpose(0, 2, 1, 3).reshape(L * TT, L * TT)
        projected_field = jnp.dot(collocation_matrix, density_delta, preferred_element_type=jnp.float32).astype(jnp.bfloat16)
        diff = tile_placement[:, :, None] - tile_placement[:, None, :]
        dist2 = lax.optimization_barrier(jnp.sum(diff * diff, axis=0))
        exchange_kernel = (quadrature_weight[:, None] * quadrature_weight[None, :] / jnp.sqrt(dist2 + SOFTEN * SOFTEN)).astype(jnp.bfloat16)
        grid_field = jnp.dot(exchange_kernel, projected_field, preferred_element_type=jnp.float32).astype(jnp.bfloat16)
        full_exchange = jnp.dot(collocation_matrix.T, grid_field, preferred_element_type=jnp.float32)
        ktiles = full_exchange.reshape(L, TT, L, TT).transpose(0, 2, 1, 3).reshape(L * L, TT, TT)
        ktiles = jnp.where(live_pair[:, None, None], ktiles, 0.0)
        return (pool.at[index].add(ktiles), None)
    start = jnp.zeros((TILES, TT, TT), jnp.float32)
    total, _ = lax.scan(batch_term, start, (collocation, coords, weights, owners, slots, counts))
    return fock_prev.astype(jnp.float32) - 0.5 * total
```

```python
import functools

import jax
import jax.numpy as jnp
from jax import lax
from jax.experimental import pallas as pl
from jax.experimental.pallas import tpu as pltpu
from jax.sharding import PartitionSpec as P

SOFTEN = 0.5
VMEM_BYTES = 48 * 2**20


def metric_kernel(colloc_ref, coords_ref, weights_ref, metric_ref):
    points = colloc_ref.shape[0]
    xyz = coords_ref[...]
    w = weights_ref[...]
    rows = jnp.concatenate([xyz, w, jnp.zeros((4, points), jnp.float32)], axis=0)
    cols = rows.T
    a = colloc_ref[...]
    total = jnp.full((points, points), SOFTEN * SOFTEN, jnp.float32)
    for axis in range(3):
        diff = cols[:, axis : axis + 1] - xyz[axis : axis + 1, :]
        total = total + diff * diff
    kern = (cols[:, 3:4] * w * lax.rsqrt(total)).astype(jnp.bfloat16)
    smeared = jnp.dot(kern, a, preferred_element_type=jnp.float32).astype(jnp.bfloat16)
    metric_ref[...] = lax.dot_general(
        a, smeared, (((0,), (0,)), ((), ())), preferred_element_type=jnp.float32
    ).astype(jnp.bfloat16)


def metric_of(collocation, coords, weights):
    per_dev, points, funcs = collocation.shape
    return pl.pallas_call(
        metric_kernel,
        grid=(per_dev,),
        out_shape=jax.ShapeDtypeStruct((per_dev, funcs, funcs), jnp.bfloat16),
        in_specs=[
            pl.BlockSpec((None, points, funcs), lambda b: (b, 0, 0)),
            pl.BlockSpec((None, 3, points), lambda b: (b, 0, 0)),
            pl.BlockSpec((None, 1, points), lambda b: (b, 0, 0)),
        ],
        out_specs=pl.BlockSpec((None, funcs, funcs), lambda b: (b, 0, 0)),
        compiler_params=pltpu.CompilerParams(vmem_limit_bytes=VMEM_BYTES),
        cost_estimate=pl.CostEstimate(
            flops=4 * per_dev * points * points * funcs,
            bytes_accessed=4 * per_dev * points * funcs,
            transcendentals=per_dev * points * points,
        ),
        name="metric",
    )(collocation, coords, weights[:, None, :])


def pick_kernel(asked_ref, scales_ref, dens_ref, out_ref, scaled):
    stored = dens_ref.shape[0]
    count = out_ref.shape[0]
    step = pl.program_id(0)

    @pl.when(step == 0)
    def _():
        def one(t, carry):
            scaled[t] = (dens_ref[t].astype(jnp.float32) * scales_ref[t]).astype(jnp.bfloat16)
            return carry

        lax.fori_loop(0, stored, one, 0)

    for k in range(count):
        out_ref[k] = scaled[asked_ref[step * count + k]]


def pick(asked, scales, dens, chunk):
    total = asked.shape[0]
    stored, width, _ = dens.shape
    return pl.pallas_call(
        pick_kernel,
        out_shape=jax.ShapeDtypeStruct((total, width, width), jnp.bfloat16),
        grid_spec=pltpu.PrefetchScalarGridSpec(
            num_scalar_prefetch=2,
            grid=(total // chunk,),
            in_specs=[pl.BlockSpec((stored, width, width), lambda s, *_: (0, 0, 0))],
            out_specs=pl.BlockSpec((chunk, width, width), lambda s, *_: (s, 0, 0)),
            scratch_shapes=[pltpu.VMEM((stored, width, width), jnp.bfloat16)],
        ),
        compiler_params=pltpu.CompilerParams(vmem_limit_bytes=VMEM_BYTES),
        name="pick",
    )(asked, scales, dens)


def apply_kernel(listed, pos_ref, counts_ref, fetched_ref, metric_ref, out_ref, dmat):
    width = fetched_ref.shape[1]
    b = pl.program_id(0)
    count = counts_ref[b]
    for i in range(listed):
        for j in range(listed):
            live = max(i, j) < count
            where = pos_ref[b * listed * listed + i * listed + j]
            tile = fetched_ref[where]
            dmat[i * width : (i + 1) * width, j * width : (j + 1) * width] = jnp.where(
                live, tile, jnp.zeros_like(tile)
            )
    parts = jnp.dot(metric_ref[...], dmat[...], preferred_element_type=jnp.float32)
    for i in range(listed):
        for j in range(listed):
            live = max(i, j) < count
            where = pos_ref[b * listed * listed + i * listed + j]
            part = parts[i * width : (i + 1) * width, j * width : (j + 1) * width]
            part = part.astype(jnp.bfloat16)
            out_ref[where] = jnp.where(live, part, jnp.zeros_like(part))


def apply_metric(pos, counts, fetched, metric):
    total, width, _ = fetched.shape
    per_dev, funcs, _ = metric.shape
    return pl.pallas_call(
        functools.partial(apply_kernel, funcs // width),
        out_shape=jax.ShapeDtypeStruct((total, width, width), jnp.bfloat16),
        grid_spec=pltpu.PrefetchScalarGridSpec(
            num_scalar_prefetch=2,
            grid=(per_dev,),
            in_specs=[
                pl.BlockSpec(
                    (total, width, width), lambda b, *_: (0, 0, 0), pipeline_mode=pl.Buffered(1)
                ),
                pl.BlockSpec((None, funcs, funcs), lambda b, *_: (b, 0, 0)),
            ],
            out_specs=pl.BlockSpec((total, width, width), lambda b, *_: (0, 0, 0)),
            scratch_shapes=[pltpu.VMEM((funcs, funcs), jnp.bfloat16)],
        ),
        compiler_params=pltpu.CompilerParams(vmem_limit_bytes=VMEM_BYTES),
        name="apply_metric",
    )(pos, counts, fetched, metric)


def update_kernel(asked_ref, received_ref, prev_ref, out_ref):
    count = received_ref.shape[0]
    step = pl.program_id(0)

    @pl.when(step == 0)
    def _():
        out_ref[...] = prev_ref[...].astype(jnp.float32)

    for k in range(count):
        slot = asked_ref[step * count + k]
        out_ref[slot] = out_ref[slot] - 0.5 * received_ref[k].astype(jnp.float32)


def update(asked, received, prev, chunk):
    total, width, _ = received.shape
    stored = prev.shape[0]
    return pl.pallas_call(
        update_kernel,
        out_shape=jax.ShapeDtypeStruct((stored, width, width), jnp.float32),
        grid_spec=pltpu.PrefetchScalarGridSpec(
            num_scalar_prefetch=1,
            grid=(total // chunk,),
            in_specs=[
                pl.BlockSpec((chunk, width, width), lambda s, *_: (s, 0, 0)),
                pl.BlockSpec((stored, width, width), lambda s, *_: (0, 0, 0)),
            ],
            out_specs=pl.BlockSpec((stored, width, width), lambda s, *_: (0, 0, 0)),
        ),
        compiler_params=pltpu.CompilerParams(vmem_limit_bytes=VMEM_BYTES),
        name="update",
    )(asked, received, prev)


def shards(collocation, coords, weights, owners, slots, counts, dens_tiles, dens_scales, fock_prev):
    npeer = lax.axis_size("grid")
    per_dev, npair = owners.shape
    width = dens_tiles.shape[1]
    entries = per_dev * npair
    capacity = entries // npeer
    flat_owner = owners.reshape(-1)
    flat_slot = slots.reshape(-1)
    onehot = (flat_owner[:, None] == jnp.arange(npeer, dtype=jnp.int32)[None, :]).astype(jnp.bfloat16)
    before = jnp.tril(jnp.ones((entries, entries), jnp.bfloat16), -1)
    running = jnp.dot(before, onehot, preferred_element_type=jnp.float32)
    rank = jnp.sum(running * onehot.astype(jnp.float32), axis=1).astype(jnp.int32)
    pos = flat_owner * capacity + rank
    ranked = jnp.where(
        rank[:, None] == jnp.arange(capacity, dtype=jnp.int32)[None, :], flat_slot[:, None], 0
    )
    requests = jnp.dot(
        onehot.T, ranked.astype(jnp.bfloat16), preferred_element_type=jnp.float32
    ).astype(jnp.int32)
    asked = lax.all_to_all(requests, "grid", split_axis=0, concat_axis=0, tiled=True).reshape(-1)
    chunk = 16
    tiles = pick(asked, dens_scales, dens_tiles, chunk)
    metric = metric_of(collocation, coords, weights)
    fetched = lax.all_to_all(
        tiles.reshape(npeer, capacity, width, width), "grid", split_axis=0, concat_axis=0, tiled=True
    ).reshape(entries, width, width)
    outgoing = apply_metric(pos, counts, fetched, metric)
    received = lax.all_to_all(
        outgoing.reshape(npeer, capacity, width, width), "grid", split_axis=0, concat_axis=0, tiled=True
    ).reshape(entries, width, width)
    return update(asked, received, fock_prev, chunk)


def solution(mesh):
    split = ("groups", "grid")
    return jax.shard_map(
        shards,
        mesh=mesh,
        in_specs=(
            P(split, None, None),
            P(split, None, None),
            P(split, None),
            P(split, None),
            P(split, None),
            P(split),
            P(split, None, None),
            P(split),
            P(split, None, None),
        ),
        out_specs=P(split, None, None),
        check_vma=False,
    )
```

```python
import functools

import jax
import jax.numpy as jnp
from jax import lax
from jax.experimental import pallas as pl
from jax.experimental.pallas import tpu as pltpu
from jax.sharding import PartitionSpec as P

SOFTEN = 0.5
VMEM_BYTES = 48 * 2**20


def metric_kernel(colloc_ref, coords_ref, weights_ref, metric_ref):
    points = colloc_ref.shape[0]
    xyz = coords_ref[...]
    w = weights_ref[...]
    rows = jnp.concatenate([xyz, w, jnp.zeros((4, points), jnp.float32)], axis=0)
    cols = rows.T
    a = colloc_ref[...]
    total = jnp.full((points, points), SOFTEN * SOFTEN, jnp.float32)
    for axis in range(3):
        diff = cols[:, axis : axis + 1] - xyz[axis : axis + 1, :]
        total = total + diff * diff
    kern = (cols[:, 3:4] * w * lax.rsqrt(total)).astype(jnp.bfloat16)
    smeared = jnp.dot(kern, a, preferred_element_type=jnp.float32).astype(jnp.bfloat16)
    metric_ref[...] = lax.dot_general(
        a, smeared, (((0,), (0,)), ((), ())), preferred_element_type=jnp.float32
    ).astype(jnp.bfloat16)


def metric_of(collocation, coords, weights):
    per_dev, points, funcs = collocation.shape
    return pl.pallas_call(
        metric_kernel,
        grid=(per_dev,),
        out_shape=jax.ShapeDtypeStruct((per_dev, funcs, funcs), jnp.bfloat16),
        in_specs=[
            pl.BlockSpec((None, points, funcs), lambda b: (b, 0, 0)),
            pl.BlockSpec((None, 3, points), lambda b: (b, 0, 0)),
            pl.BlockSpec((None, 1, points), lambda b: (b, 0, 0)),
        ],
        out_specs=pl.BlockSpec((None, funcs, funcs), lambda b: (b, 0, 0)),
        compiler_params=pltpu.CompilerParams(vmem_limit_bytes=VMEM_BYTES),
        cost_estimate=pl.CostEstimate(
            flops=4 * per_dev * points * points * funcs,
            bytes_accessed=4 * per_dev * points * funcs,
            transcendentals=per_dev * points * points,
        ),
        name="metric",
    )(collocation, coords, weights[:, None, :])


def pick_kernel(asked_ref, scales_ref, dens_ref, out_ref, scaled):
    stored = dens_ref.shape[0]
    count = out_ref.shape[0]
    step = pl.program_id(0)

    @pl.when(step == 0)
    def _():
        def one(t, carry):
            scaled[t] = (dens_ref[t].astype(jnp.float32) * scales_ref[t]).astype(jnp.bfloat16)
            return carry

        lax.fori_loop(0, stored, one, 0)

    for k in range(count):
        out_ref[k] = scaled[asked_ref[step * count + k]]


def pick(asked, scales, dens, chunk):
    total = asked.shape[0]
    stored, width, _ = dens.shape
    return pl.pallas_call(
        pick_kernel,
        out_shape=jax.ShapeDtypeStruct((total, width, width), jnp.bfloat16),
        grid_spec=pltpu.PrefetchScalarGridSpec(
            num_scalar_prefetch=2,
            grid=(total // chunk,),
            in_specs=[pl.BlockSpec((stored, width, width), lambda s, *_: (0, 0, 0))],
            out_specs=pl.BlockSpec((chunk, width, width), lambda s, *_: (s, 0, 0)),
            scratch_shapes=[pltpu.VMEM((stored, width, width), jnp.bfloat16)],
        ),
        compiler_params=pltpu.CompilerParams(vmem_limit_bytes=VMEM_BYTES),
        name="pick",
    )(asked, scales, dens)


def apply_kernel(listed, pos_ref, counts_ref, fetched_ref, metric_ref, out_ref, dmat):
    width = fetched_ref.shape[1]
    b = pl.program_id(0)
    count = counts_ref[b]
    for i in range(listed):
        for j in range(listed):
            live = max(i, j) < count
            where = pos_ref[b * listed * listed + i * listed + j]
            tile = fetched_ref[where]
            dmat[i * width : (i + 1) * width, j * width : (j + 1) * width] = jnp.where(
                live, tile, jnp.zeros_like(tile)
            )
    parts = jnp.dot(metric_ref[...], dmat[...], preferred_element_type=jnp.float32)
    for i in range(listed):
        for j in range(listed):
            live = max(i, j) < count
            where = pos_ref[b * listed * listed + i * listed + j]
            part = parts[i * width : (i + 1) * width, j * width : (j + 1) * width]
            part = part.astype(jnp.bfloat16)
            out_ref[where] = jnp.where(live, part, jnp.zeros_like(part))


def apply_metric(pos, counts, fetched, metric):
    total, width, _ = fetched.shape
    per_dev, funcs, _ = metric.shape
    return pl.pallas_call(
        functools.partial(apply_kernel, funcs // width),
        out_shape=jax.ShapeDtypeStruct((total, width, width), jnp.bfloat16),
        grid_spec=pltpu.PrefetchScalarGridSpec(
            num_scalar_prefetch=2,
            grid=(per_dev,),
            in_specs=[
                pl.BlockSpec(
                    (total, width, width), lambda b, *_: (0, 0, 0), pipeline_mode=pl.Buffered(1)
                ),
                pl.BlockSpec((None, funcs, funcs), lambda b, *_: (b, 0, 0)),
            ],
            out_specs=pl.BlockSpec((total, width, width), lambda b, *_: (0, 0, 0)),
            scratch_shapes=[pltpu.VMEM((funcs, funcs), jnp.bfloat16)],
        ),
        compiler_params=pltpu.CompilerParams(vmem_limit_bytes=VMEM_BYTES),
        name="apply_metric",
    )(pos, counts, fetched, metric)


def update_kernel(asked_ref, received_ref, prev_ref, out_ref):
    count = received_ref.shape[0]
    step = pl.program_id(0)

    @pl.when(step == 0)
    def _():
        out_ref[...] = prev_ref[...].astype(jnp.float32)

    for k in range(count):
        slot = asked_ref[step * count + k]
        out_ref[slot] = out_ref[slot] - 0.5 * received_ref[k].astype(jnp.float32)


def update(asked, received, prev, chunk):
    total, width, _ = received.shape
    stored = prev.shape[0]
    return pl.pallas_call(
        update_kernel,
        out_shape=jax.ShapeDtypeStruct((stored, width, width), jnp.float32),
        grid_spec=pltpu.PrefetchScalarGridSpec(
            num_scalar_prefetch=1,
            grid=(total // chunk,),
            in_specs=[
                pl.BlockSpec((chunk, width, width), lambda s, *_: (s, 0, 0)),
                pl.BlockSpec((stored, width, width), lambda s, *_: (0, 0, 0)),
            ],
            out_specs=pl.BlockSpec((stored, width, width), lambda s, *_: (0, 0, 0)),
        ),
        compiler_params=pltpu.CompilerParams(vmem_limit_bytes=VMEM_BYTES),
        name="update",
    )(asked, received, prev)


def mate(z, lane, plane):
    return {"grid": z * plane + lane}


def greet(z, q, plane, line):
    barrier = pltpu.get_barrier_semaphore()
    for k in range(1, plane):
        pl.semaphore_signal(
            barrier, inc=1, device_id=mate(z, lax.rem(q + k, plane), plane), device_id_type=pl.DeviceIdType.MESH
        )

    @pl.when(z > 0)
    def _():
        pl.semaphore_signal(barrier, inc=1, device_id=mate(z - 1, q, plane), device_id_type=pl.DeviceIdType.MESH)

    @pl.when(z < line - 1)
    def _():
        pl.semaphore_signal(barrier, inc=1, device_id=mate(z + 1, q, plane), device_id_type=pl.DeviceIdType.MESH)

    pl.semaphore_wait(barrier, plane - 1 + jnp.where(z > 0, 1, 0) + jnp.where(z < line - 1, 1, 0))


def fetch_kernel(
    plane, line, asked_ref, scales_ref, dens_ref, colloc_ref, coords_ref, weights_ref, fetched_ref, metric_ref,
    *scratch
):
    pools, (stage, hop_send, hop_recv, local_sem, send_sem, recv_sem) = scratch[:line], scratch[line:]
    capacity = fetched_ref.shape[1]
    stored = dens_ref.shape[0]
    batches = colloc_ref.shape[0]
    me = lax.axis_index("grid")
    z, q = me // plane, lax.rem(me, plane)

    def scale(t, carry):
        pools[0][t] = (dens_ref[t].astype(jnp.float32) * scales_ref[t]).astype(jnp.bfloat16)
        return carry

    lax.fori_loop(0, stored, scale, 0)
    greet(z, q, plane, line)

    def hop(slot, up):
        to_slot = (slot + 1 if up else slot - 1) % line
        return pltpu.make_async_remote_copy(
            src_ref=pools[slot],
            dst_ref=pools[to_slot],
            send_sem=hop_send.at[line if (slot == 0 and not up) else slot],
            recv_sem=hop_recv.at[to_slot],
            device_id=mate(z + 1 if up else z - 1, q, plane),
            device_id_type=pl.DeviceIdType.MESH,
        )

    def hops(slot, act):
        if slot + 1 < line:

            @pl.when((z >= slot) & (z < line - 1))
            def _():
                act(hop(slot, True))

        if slot != 1:

            @pl.when(((z < slot) | (slot == 0)) & (z > 0))
            def _():
                act(hop(slot, False))

    def to_mate(slot, k):
        owner = lax.rem(z - slot + line, line) * plane + q
        return pltpu.make_async_remote_copy(
            src_ref=stage.at[slot, k],
            dst_ref=fetched_ref.at[owner],
            send_sem=send_sem.at[slot, k],
            recv_sem=recv_sem.at[slot, k],
            device_id=mate(z, lax.rem(q + k, plane), plane),
            device_id_type=pl.DeviceIdType.MESH,
        )

    def to_self(slot):
        owner = lax.rem(z - slot + line, line) * plane + q
        return pltpu.make_async_copy(stage.at[slot, 0], fetched_ref.at[owner], local_sem.at[slot])

    def serve(slot):
        if slot:
            hop(slot - 1, True).wait_recv()
        hops(slot, lambda copy: copy.start())
        source = lax.rem(z - slot + line, line)

        def fill(k):
            base = (lax.rem(q + k, plane) * line + source) * capacity
            for r in range(capacity):
                stage[slot, k, r] = pools[slot][asked_ref[base + r]]

        def one(k, carry):
            fill(k)
            to_mate(slot, k).start()
            return carry

        lax.fori_loop(1, plane, one, 0)
        fill(0)
        to_self(slot).start()

    def metrics(first, last):
        def one(b, carry):
            metric_kernel(colloc_ref.at[b], coords_ref.at[b], weights_ref.at[b], metric_ref.at[b])
            return carry

        lax.fori_loop(first, last, one, 0)

    serve(0)
    for d in range(1, line):
        metrics(batches * (d - 1) // (line - 1), batches * d // (line - 1))
        if 2 * d == line:
            serve(d)
        else:
            pl.when(z >= d)(functools.partial(serve, d))
            pl.when(z + d < line)(functools.partial(serve, line - d))
    for slot in range(line):
        hops(slot, lambda copy: copy.wait_send())
        to_self(slot).wait()

        def finish(k, carry):
            to_mate(slot, k).wait()
            return carry

        lax.fori_loop(1, plane, finish, 0)


def fetch(asked, scales, dens, collocation, coords, weights, plane, line, capacity):
    stored, width, _ = dens.shape
    per_dev, points, funcs = collocation.shape
    vmem, smem = pl.BlockSpec(memory_space=pltpu.VMEM), pl.BlockSpec(memory_space=pltpu.SMEM)
    return pl.pallas_call(
        functools.partial(fetch_kernel, plane, line),
        out_shape=(
            jax.ShapeDtypeStruct((line * plane, capacity, width, width), jnp.bfloat16),
            jax.ShapeDtypeStruct((per_dev, funcs, funcs), jnp.bfloat16),
        ),
        in_specs=[smem, smem, vmem, vmem, vmem, vmem],
        out_specs=(pl.BlockSpec(memory_space=pl.ANY), vmem),
        scratch_shapes=[pltpu.VMEM((stored, width, width), jnp.bfloat16)] * line
        + [
            pltpu.VMEM((line, plane, capacity, width, width), jnp.bfloat16),
            pltpu.SemaphoreType.DMA((line + 1,)),
            pltpu.SemaphoreType.DMA((line,)),
            pltpu.SemaphoreType.DMA((line,)),
            pltpu.SemaphoreType.DMA((line, plane)),
            pltpu.SemaphoreType.DMA((line, plane)),
        ],
        compiler_params=pltpu.CompilerParams(
            collective_id=0, has_side_effects=True, vmem_limit_bytes=VMEM_BYTES
        ),
        name="fetch",
    )(asked, scales, dens, collocation, coords, weights[:, None, :])


def return_kernel(
    plane, line, perm_ref, same_ref, last_ref, has_ref, outgoing_ref, prev_ref, out_ref, *scratch
):
    received, rest = scratch[:line], scratch[line:]
    running, part, inbox, hop_send, hop_recv, local_sem, send_sem, recv_sem = rest
    capacity = outgoing_ref.shape[1]
    stored, width, _ = prev_ref.shape
    entries = plane * capacity
    me = lax.axis_index("grid")
    z, q = me // plane, lax.rem(me, plane)
    order = [jnp.where(z == 0, line - 1 - p, jnp.where(z == line - 1, (p + 1) % line, (2, 1, 3, 0)[p])) for p in range(line)]
    greet(z, q, plane, line)

    def to_mate(p, k):
        to = lax.rem(q + k, plane)
        return pltpu.make_async_remote_copy(
            src_ref=outgoing_ref.at[lax.rem(z + order[p], line) * plane + to],
            dst_ref=received[p].at[pl.ds(q * capacity, capacity)],
            send_sem=send_sem.at[p, k],
            recv_sem=recv_sem.at[p, k],
            device_id=mate(z, to, plane),
            device_id_type=pl.DeviceIdType.MESH,
        )

    def to_self(p):
        return pltpu.make_async_copy(
            outgoing_ref.at[lax.rem(z + order[p], line) * plane + q],
            received[p].at[pl.ds(q * capacity, capacity)],
            local_sem.at[p],
        )

    def exchange(p):
        def one(k, carry):
            to_mate(p, k).start()
            return carry

        lax.fori_loop(1, plane, one, 0)
        to_self(p).start()

    def hop(p, up):
        to = order[p] - 1 if up else order[p] + 1
        return pltpu.make_async_remote_copy(
            src_ref=part.at[p],
            dst_ref=inbox.at[to],
            send_sem=hop_send.at[p],
            recv_sem=hop_recv.at[to],
            device_id=mate(z + 1 if up else z - 1, q, plane),
            device_id_type=pl.DeviceIdType.MESH,
        )

    def arrival(slot):
        return pltpu.make_async_remote_copy(
            src_ref=part.at[0],
            dst_ref=inbox.at[slot],
            send_sem=hop_send.at[0],
            recv_sem=hop_recv.at[slot],
            device_id=mate(z, lax.rem(q + 1, plane), plane),
            device_id_type=pl.DeviceIdType.MESH,
        )

    def gather(p):
        def finish(k, carry):
            to_mate(p, k).wait()
            return carry

        lax.fori_loop(1, plane, finish, 0)
        to_self(p).wait()
        if p + 2 < line:
            exchange(p + 2)
        row = lax.rem(z + order[p], line)

        def one(k, total):
            tile = received[p][perm_ref[row * entries + k]].astype(jnp.float32)
            total = jnp.where(same_ref[row * entries + k] != 0, total, 0.0) + tile
            running[k] = total
            return total

        lax.fori_loop(0, entries, one, jnp.zeros((width, width), jnp.float32))

    def slot_sum(p, t):
        row = lax.rem(z + order[p], line)
        return jnp.where(has_ref[row * stored + t] != 0, running[last_ref[row * stored + t]], 0.0)

    def each(body):
        def one(t, carry):
            body(t)
            return carry

        lax.fori_loop(0, stored, one, 0)

    exchange(0)
    exchange(1)
    for p in range(line - 1):
        gather(p)
        up = z + order[p] < line
        feeds = jnp.where(up, z > 0, z < line - 1)

        @pl.when(feeds)
        def _():
            arrival(order[p]).wait_recv()

            def body(t):
                part[p, t] = (slot_sum(p, t) + inbox[order[p], t].astype(jnp.float32)).astype(jnp.bfloat16)

            each(body)

        @pl.when(jnp.logical_not(feeds))
        def _():
            def body(t):
                part[p, t] = slot_sum(p, t).astype(jnp.bfloat16)

            each(body)

        pl.when(up)(lambda: hop(p, True).start())
        pl.when(jnp.logical_not(up))(lambda: hop(p, False).start())
    gather(line - 1)

    def first(t):
        out_ref[t] = prev_ref[t].astype(jnp.float32) - 0.5 * slot_sum(line - 1, t)

    each(first)
    for slot, there in ((0, z > 0), (line, z < line - 1)):

        @pl.when(there)
        def _():
            arrival(slot).wait_recv()

            def body(t):
                out_ref[t] = out_ref[t] - 0.5 * inbox[slot, t].astype(jnp.float32)

            each(body)

    for p in range(line - 1):
        arrival_of = pltpu.make_async_remote_copy(
            src_ref=part.at[p],
            dst_ref=inbox.at[0],
            send_sem=hop_send.at[p],
            recv_sem=hop_recv.at[0],
            device_id=mate(z, lax.rem(q + 1, plane), plane),
            device_id_type=pl.DeviceIdType.MESH,
        )
        arrival_of.wait_send()


def give_back(tables, outgoing, prev, plane, line):
    stored, width, _ = prev.shape
    capacity = outgoing.shape[1]
    vmem, smem = pl.BlockSpec(memory_space=pltpu.VMEM), pl.BlockSpec(memory_space=pltpu.SMEM)
    return pl.pallas_call(
        functools.partial(return_kernel, plane, line),
        out_shape=jax.ShapeDtypeStruct((stored, width, width), jnp.float32),
        in_specs=[smem, smem, smem, smem, pl.BlockSpec(memory_space=pl.ANY), vmem],
        out_specs=vmem,
        scratch_shapes=[pltpu.VMEM((plane * capacity, width, width), jnp.bfloat16)] * line
        + [
            pltpu.VMEM((plane * capacity, width, width), jnp.float32),
            pltpu.VMEM((line - 1, stored, width, width), jnp.bfloat16),
            pltpu.VMEM((line + 1, stored, width, width), jnp.bfloat16),
            pltpu.SemaphoreType.DMA((line - 1,)),
            pltpu.SemaphoreType.DMA((line + 1,)),
            pltpu.SemaphoreType.DMA((line,)),
            pltpu.SemaphoreType.DMA((line, plane)),
            pltpu.SemaphoreType.DMA((line, plane)),
        ],
        compiler_params=pltpu.CompilerParams(
            collective_id=1, has_side_effects=True, vmem_limit_bytes=VMEM_BYTES
        ),
        name="give_back",
    )(*tables, outgoing, prev)


def slot_tables(asked, stored):
    entries = asked.shape[1]
    index = jnp.arange(entries, dtype=jnp.int32)
    earlier = (asked[:, None, :] < asked[:, :, None]) | (
        (asked[:, None, :] == asked[:, :, None]) & (index[None, None, :] < index[None, :, None])
    )
    place = jnp.sum(earlier.astype(jnp.int32), axis=2)
    at = place[:, None, :] == index[None, :, None]
    perm = jnp.sum(jnp.where(at, index[None, None, :], 0), axis=2)
    shared = jnp.any(
        (asked[:, None, :] == asked[:, :, None]) & (index[None, None, :] < index[None, :, None]), axis=2
    )
    same = jnp.sum((at & shared[:, None, :]).astype(jnp.int32), axis=2)
    slot = jnp.arange(stored, dtype=jnp.int32)[None, :, None]
    last = jnp.maximum(jnp.sum((asked[:, None, :] <= slot).astype(jnp.int32), axis=2) - 1, 0)
    has = jnp.any(asked[:, None, :] == slot, axis=2).astype(jnp.int32)
    return tuple(table.reshape(-1) for table in (perm, same, last, has))


def shards(collocation, coords, weights, owners, slots, counts, dens_tiles, dens_scales, fock_prev):
    npeer = lax.axis_size("grid")
    per_dev, npair = owners.shape
    width = dens_tiles.shape[1]
    entries = per_dev * npair
    capacity = entries // npeer
    flat_owner = owners.reshape(-1)
    flat_slot = slots.reshape(-1)
    onehot = (flat_owner[:, None] == jnp.arange(npeer, dtype=jnp.int32)[None, :]).astype(jnp.bfloat16)
    before = jnp.tril(jnp.ones((entries, entries), jnp.bfloat16), -1)
    running = jnp.dot(before, onehot, preferred_element_type=jnp.float32)
    rank = jnp.sum(running * onehot.astype(jnp.float32), axis=1).astype(jnp.int32)
    pos = flat_owner * capacity + rank
    ranked = jnp.where(
        rank[:, None] == jnp.arange(capacity, dtype=jnp.int32)[None, :], flat_slot[:, None], 0
    )
    requests = jnp.dot(
        onehot.T, ranked.astype(jnp.bfloat16), preferred_element_type=jnp.float32
    ).astype(jnp.int32)
    plane = 8
    line = npeer // plane
    if line == 4:
        wanted = requests.reshape(line, plane, capacity).transpose(1, 0, 2)
        groups = [[z * plane + k for k in range(plane)] for z in range(line)]
        asked = lax.all_to_all(
            wanted, "grid", split_axis=0, concat_axis=0, tiled=True, axis_index_groups=groups
        )
        tables = slot_tables(asked.transpose(1, 0, 2).reshape(line, plane * capacity), dens_tiles.shape[0])
        fetched, metric = fetch(
            asked.reshape(-1), dens_scales, dens_tiles, collocation, coords, weights, plane, line, capacity
        )
        outgoing = apply_metric(pos, counts, fetched.reshape(entries, width, width), metric)
        return give_back(tables, outgoing.reshape(npeer, capacity, width, width), fock_prev, plane, line)
    asked = lax.all_to_all(requests, "grid", split_axis=0, concat_axis=0, tiled=True).reshape(-1)
    chunk = 16
    tiles = pick(asked, dens_scales, dens_tiles, chunk)
    metric = metric_of(collocation, coords, weights)
    fetched = lax.all_to_all(
        tiles.reshape(npeer, capacity, width, width), "grid", split_axis=0, concat_axis=0, tiled=True
    ).reshape(entries, width, width)
    outgoing = apply_metric(pos, counts, fetched, metric)
    received = lax.all_to_all(
        outgoing.reshape(npeer, capacity, width, width), "grid", split_axis=0, concat_axis=0, tiled=True
    ).reshape(entries, width, width)
    return update(asked, received, fock_prev, chunk)


def solution(mesh):
    split = ("groups", "grid")
    return jax.shard_map(
        shards,
        mesh=mesh,
        in_specs=(
            P(split, None, None),
            P(split, None, None),
            P(split, None),
            P(split, None),
            P(split, None),
            P(split),
            P(split, None, None),
            P(split),
            P(split, None, None),
        ),
        out_specs=P(split, None, None),
        check_vma=False,
    )
```

```python
import functools

import jax
import jax.numpy as jnp
from jax import lax
from jax.experimental import pallas as pl
from jax.experimental.pallas import tpu as pltpu
from jax.sharding import PartitionSpec as P

SOFTEN = 0.5
VMEM_BYTES = 48 * 2**20


def metric_kernel(colloc_ref, coords_ref, weights_ref, metric_ref):
    points = colloc_ref.shape[0]
    xyz = coords_ref[...]
    w = weights_ref[...]
    rows = jnp.concatenate([xyz, w, jnp.zeros((4, points), jnp.float32)], axis=0)
    cols = rows.T
    a = colloc_ref[...]
    total = jnp.full((points, points), SOFTEN * SOFTEN, jnp.float32)
    for axis in range(3):
        diff = cols[:, axis : axis + 1] - xyz[axis : axis + 1, :]
        total = total + diff * diff
    kern = (cols[:, 3:4] * w * lax.rsqrt(total)).astype(jnp.bfloat16)
    smeared = jnp.dot(kern, a, preferred_element_type=jnp.float32).astype(jnp.bfloat16)
    metric_ref[...] = lax.dot_general(
        a, smeared, (((0,), (0,)), ((), ())), preferred_element_type=jnp.float32
    ).astype(jnp.bfloat16)


def metric_of(collocation, coords, weights):
    per_dev, points, funcs = collocation.shape
    return pl.pallas_call(
        metric_kernel,
        grid=(per_dev,),
        out_shape=jax.ShapeDtypeStruct((per_dev, funcs, funcs), jnp.bfloat16),
        in_specs=[
            pl.BlockSpec((None, points, funcs), lambda b: (b, 0, 0)),
            pl.BlockSpec((None, 3, points), lambda b: (b, 0, 0)),
            pl.BlockSpec((None, 1, points), lambda b: (b, 0, 0)),
        ],
        out_specs=pl.BlockSpec((None, funcs, funcs), lambda b: (b, 0, 0)),
        compiler_params=pltpu.CompilerParams(vmem_limit_bytes=VMEM_BYTES),
        cost_estimate=pl.CostEstimate(
            flops=4 * per_dev * points * points * funcs,
            bytes_accessed=4 * per_dev * points * funcs,
            transcendentals=per_dev * points * points,
        ),
        name="metric",
    )(collocation, coords, weights[:, None, :])


def pick_kernel(asked_ref, scales_ref, dens_ref, out_ref, scaled):
    stored = dens_ref.shape[0]
    count = out_ref.shape[0]
    step = pl.program_id(0)

    @pl.when(step == 0)
    def _():
        def one(t, carry):
            scaled[t] = (dens_ref[t].astype(jnp.float32) * scales_ref[t]).astype(jnp.bfloat16)
            return carry

        lax.fori_loop(0, stored, one, 0)

    for k in range(count):
        out_ref[k] = scaled[asked_ref[step * count + k]]


def pick(asked, scales, dens, chunk):
    total = asked.shape[0]
    stored, width, _ = dens.shape
    return pl.pallas_call(
        pick_kernel,
        out_shape=jax.ShapeDtypeStruct((total, width, width), jnp.bfloat16),
        grid_spec=pltpu.PrefetchScalarGridSpec(
            num_scalar_prefetch=2,
            grid=(total // chunk,),
            in_specs=[pl.BlockSpec((stored, width, width), lambda s, *_: (0, 0, 0))],
            out_specs=pl.BlockSpec((chunk, width, width), lambda s, *_: (s, 0, 0)),
            scratch_shapes=[pltpu.VMEM((stored, width, width), jnp.bfloat16)],
        ),
        compiler_params=pltpu.CompilerParams(vmem_limit_bytes=VMEM_BYTES),
        name="pick",
    )(asked, scales, dens)


def apply_kernel(listed, pos_ref, counts_ref, fetched_ref, metric_ref, out_ref, dmat):
    width = fetched_ref.shape[1]
    b = pl.program_id(0)
    count = jnp.clip(counts_ref[b], 0, listed)

    def at(i, j):
        return pos_ref[b * listed * listed + i * listed + j]

    def live(size):
        for i in range(size):
            for j in range(size):
                dmat[i * width : (i + 1) * width, j * width : (j + 1) * width] = fetched_ref[at(i, j)]
        span = size * width
        for i in range(size):
            parts = jnp.dot(
                metric_ref[i * width : (i + 1) * width, :span], dmat[:span, :span], preferred_element_type=jnp.float32
            ).astype(jnp.bfloat16)
            for j in range(size):
                out_ref[at(i, j)] = parts[:, j * width : (j + 1) * width]

    def branch(size):
        if size:
            live(size)
        for i in range(listed):
            for j in range(listed):
                if max(i, j) >= size:
                    out_ref[at(i, j)] = jnp.zeros((width, width), jnp.bfloat16)

    for size in range(listed + 1):
        pl.when(count == size)(functools.partial(branch, size))


def apply_metric(pos, counts, fetched, metric):
    total, width, _ = fetched.shape
    per_dev, funcs, _ = metric.shape
    return pl.pallas_call(
        functools.partial(apply_kernel, funcs // width),
        out_shape=jax.ShapeDtypeStruct((total, width, width), jnp.bfloat16),
        grid_spec=pltpu.PrefetchScalarGridSpec(
            num_scalar_prefetch=2,
            grid=(per_dev,),
            in_specs=[
                pl.BlockSpec(
                    (total, width, width), lambda b, *_: (0, 0, 0), pipeline_mode=pl.Buffered(1)
                ),
                pl.BlockSpec((None, funcs, funcs), lambda b, *_: (b, 0, 0)),
            ],
            out_specs=pl.BlockSpec((total, width, width), lambda b, *_: (0, 0, 0)),
            scratch_shapes=[pltpu.VMEM((funcs, funcs), jnp.bfloat16)],
        ),
        compiler_params=pltpu.CompilerParams(vmem_limit_bytes=VMEM_BYTES),
        name="apply_metric",
    )(pos, counts, fetched, metric)


def update_kernel(asked_ref, received_ref, prev_ref, out_ref):
    count = received_ref.shape[0]
    step = pl.program_id(0)

    @pl.when(step == 0)
    def _():
        out_ref[...] = prev_ref[...].astype(jnp.float32)

    for k in range(count):
        slot = asked_ref[step * count + k]
        out_ref[slot] = out_ref[slot] - 0.5 * received_ref[k].astype(jnp.float32)


def update(asked, received, prev, chunk):
    total, width, _ = received.shape
    stored = prev.shape[0]
    return pl.pallas_call(
        update_kernel,
        out_shape=jax.ShapeDtypeStruct((stored, width, width), jnp.float32),
        grid_spec=pltpu.PrefetchScalarGridSpec(
            num_scalar_prefetch=1,
            grid=(total // chunk,),
            in_specs=[
                pl.BlockSpec((chunk, width, width), lambda s, *_: (s, 0, 0)),
                pl.BlockSpec((stored, width, width), lambda s, *_: (0, 0, 0)),
            ],
            out_specs=pl.BlockSpec((stored, width, width), lambda s, *_: (0, 0, 0)),
        ),
        compiler_params=pltpu.CompilerParams(vmem_limit_bytes=VMEM_BYTES),
        name="update",
    )(asked, received, prev)


def mate(z, lane, plane):
    return {"grid": z * plane + lane}


def greet(z, q, plane, line):
    barrier = pltpu.get_barrier_semaphore()
    for k in range(1, plane):
        pl.semaphore_signal(
            barrier, inc=1, device_id=mate(z, lax.rem(q + k, plane), plane), device_id_type=pl.DeviceIdType.MESH
        )

    @pl.when(z > 0)
    def _():
        pl.semaphore_signal(barrier, inc=1, device_id=mate(z - 1, q, plane), device_id_type=pl.DeviceIdType.MESH)

    @pl.when(z < line - 1)
    def _():
        pl.semaphore_signal(barrier, inc=1, device_id=mate(z + 1, q, plane), device_id_type=pl.DeviceIdType.MESH)

    pl.semaphore_wait(barrier, plane - 1 + jnp.where(z > 0, 1, 0) + jnp.where(z < line - 1, 1, 0))


def slot_tables(asked_ref, tables_ref, line, capacity):
    entries = tables_ref.shape[2]
    row = lax.broadcasted_iota(jnp.int32, (entries, entries), 0)
    column = lax.broadcasted_iota(jnp.int32, (entries, entries), 1)

    def ones(mask):
        return jnp.where(mask, 1.0, 0.0)

    for source in range(line):

        def spread(e, carry):
            down, across = carry
            slot = asked_ref[e // capacity, 0, source * capacity + e % capacity]
            return jnp.where(row == e, slot, down), jnp.where(column == e, slot, across)

        zero = jnp.zeros((entries, entries), jnp.int32)
        mine, other = lax.fori_loop(0, entries, spread, (zero, zero))
        twin = (other == mine) & (column < row)
        place = jnp.sum(ones((other < mine) | twin), axis=1, keepdims=True)
        shared = jnp.max(ones(twin), axis=1, keepdims=True)
        at = place == column.astype(jnp.float32)
        tables_ref[source, 0:1, :] = jnp.sum(jnp.where(at, row.astype(jnp.float32), 0.0), axis=0, keepdims=True).astype(jnp.int32)
        tables_ref[source, 1:2, :] = jnp.sum(jnp.where(at, shared, 0.0), axis=0, keepdims=True).astype(jnp.int32)
        upto = jnp.sum(ones(mine <= column), axis=0, keepdims=True)
        tables_ref[source, 2:3, :] = jnp.maximum(upto - 1.0, 0.0).astype(jnp.int32)
        tables_ref[source, 3:4, :] = jnp.max(ones(mine == column), axis=0, keepdims=True).astype(jnp.int32)
        tables_ref[source, 4:8, :] = jnp.zeros((4, entries), jnp.int32)


def fetch_kernel(
    plane, line, wanted_ref, scales_ref, dens_ref, colloc_hbm, coords_ref, weights_ref, fetched_ref, metric_hbm,
    tables_ref, *scratch
):
    pools, rest = scratch[:line], scratch[line:]
    stage, colloc_ref, metric_ref, asked_vmem, asked_ref = rest[:5]
    in_sem, out_sem, smem_sem, ask_send, ask_recv, hop_send, hop_recv, local_sem, send_sem, recv_sem = rest[5:]
    capacity = fetched_ref.shape[1]
    stored = dens_ref.shape[0]
    batches = colloc_ref.shape[0]
    me = lax.axis_index("grid")
    z, q = me // plane, lax.rem(me, plane)
    load = pltpu.make_async_copy(colloc_hbm, colloc_ref, in_sem)
    load.start()

    def scale(t, carry):
        pools[0][t] = (dens_ref[t].astype(jnp.float32) * scales_ref[t]).astype(jnp.bfloat16)
        return carry

    lax.fori_loop(0, stored, scale, 0)
    greet(z, q, plane, line)

    def hop(slot, up):
        to_slot = (slot + 1 if up else slot - 1) % line
        return pltpu.make_async_remote_copy(
            src_ref=pools[slot],
            dst_ref=pools[to_slot],
            send_sem=hop_send.at[line if (slot == 0 and not up) else slot],
            recv_sem=hop_recv.at[to_slot],
            device_id=mate(z + 1 if up else z - 1, q, plane),
            device_id_type=pl.DeviceIdType.MESH,
        )

    def hops(slot, act):
        if slot + 1 < line:

            @pl.when((z >= slot) & (z < line - 1))
            def _():
                act(hop(slot, True))

        if slot != 1:

            @pl.when(((z < slot) | (slot == 0)) & (z > 0))
            def _():
                act(hop(slot, False))

    def to_mate(slot, k):
        owner = lax.rem(z - slot + line, line) * plane + q
        return pltpu.make_async_remote_copy(
            src_ref=stage.at[slot, k],
            dst_ref=fetched_ref.at[owner],
            send_sem=send_sem.at[slot, k],
            recv_sem=recv_sem.at[slot, k],
            device_id=mate(z, lax.rem(q + k, plane), plane),
            device_id_type=pl.DeviceIdType.MESH,
        )

    def to_self(slot):
        owner = lax.rem(z - slot + line, line) * plane + q
        return pltpu.make_async_copy(stage.at[slot, 0], fetched_ref.at[owner], local_sem.at[slot])

    def serve(slot):
        if slot:
            hop(slot - 1, True).wait_recv()
            hops(slot, lambda copy: copy.start())
        source = lax.rem(z - slot + line, line)

        def fill(k):
            to = lax.rem(q + k, plane)
            for r in range(capacity):
                stage[slot, k, r] = pools[slot][asked_ref[to, 0, source * capacity + r]]

        def one(k, carry):
            fill(k)
            to_mate(slot, k).start()
            return carry

        lax.fori_loop(1, plane, one, 0)
        fill(0)
        to_self(slot).start()

    def metrics(first, last):
        def one(b, carry):
            metric_kernel(colloc_ref.at[b], coords_ref.at[b], weights_ref.at[b], metric_ref.at[b])
            return carry

        lax.fori_loop(first, last, one, 0)

    def ask(k):
        return pltpu.make_async_remote_copy(
            src_ref=wanted_ref.at[lax.rem(q + k, plane)],
            dst_ref=asked_vmem.at[q],
            send_sem=ask_send.at[k],
            recv_sem=ask_recv.at[k],
            device_id=mate(z, lax.rem(q + k, plane), plane),
            device_id_type=pl.DeviceIdType.MESH,
        )

    def store_metrics(d):
        rows = pl.ds(batches * (d - 1) // (line - 1), batches * d // (line - 1) - batches * (d - 1) // (line - 1))
        return pltpu.make_async_copy(metric_ref.at[rows], metric_hbm.at[rows], out_sem.at[d])

    for k in range(1, plane):
        ask(k).start()
    own = pltpu.make_async_copy(wanted_ref.at[q], asked_vmem.at[q], ask_send.at[0])
    own.start()
    hops(0, lambda copy: copy.start())
    own.wait()
    for k in range(1, plane):
        ask(k).wait()
    scalars = pltpu.make_async_copy(asked_vmem, asked_ref, smem_sem)
    scalars.start()
    scalars.wait()
    serve(0)
    slot_tables(asked_ref, tables_ref, line, capacity)
    load.wait()
    for d in range(1, line):
        metrics(batches * (d - 1) // (line - 1), batches * d // (line - 1))
        store_metrics(d).start()
        if 2 * d == line:
            serve(d)
        else:
            pl.when(z >= d)(functools.partial(serve, d))
            pl.when(z + d < line)(functools.partial(serve, line - d))
    for d in range(1, line):
        store_metrics(d).wait()
    for slot in range(line):
        hops(slot, lambda copy: copy.wait_send())
        to_self(slot).wait()

        def finish(k, carry):
            to_mate(slot, k).wait()
            return carry

        lax.fori_loop(1, plane, finish, 0)


def fetch(wanted, scales, dens, collocation, coords, weights, plane, line, capacity):
    stored, width, _ = dens.shape
    per_dev, points, funcs = collocation.shape
    vmem, smem = pl.BlockSpec(memory_space=pltpu.VMEM), pl.BlockSpec(memory_space=pltpu.SMEM)
    hbm = pl.BlockSpec(memory_space=pl.ANY)
    return pl.pallas_call(
        functools.partial(fetch_kernel, plane, line),
        out_shape=(
            jax.ShapeDtypeStruct((line * plane, capacity, width, width), jnp.bfloat16),
            jax.ShapeDtypeStruct((per_dev, funcs, funcs), jnp.bfloat16),
            jax.ShapeDtypeStruct((line, 8, plane * capacity), jnp.int32),
        ),
        in_specs=[vmem, smem, vmem, hbm, vmem, vmem],
        out_specs=(hbm, hbm, vmem),
        scratch_shapes=[pltpu.VMEM((stored, width, width), jnp.bfloat16)] * line
        + [
            pltpu.VMEM((line, plane, capacity, width, width), jnp.bfloat16),
            pltpu.VMEM((per_dev, points, funcs), jnp.bfloat16),
            pltpu.VMEM((per_dev, funcs, funcs), jnp.bfloat16),
            pltpu.VMEM(wanted.shape, jnp.int32),
            pltpu.SMEM(wanted.shape, jnp.int32),
            pltpu.SemaphoreType.DMA,
            pltpu.SemaphoreType.DMA((line,)),
            pltpu.SemaphoreType.DMA,
            pltpu.SemaphoreType.DMA((plane,)),
            pltpu.SemaphoreType.DMA((plane,)),
            pltpu.SemaphoreType.DMA((line + 1,)),
            pltpu.SemaphoreType.DMA((line,)),
            pltpu.SemaphoreType.DMA((line,)),
            pltpu.SemaphoreType.DMA((line, plane)),
            pltpu.SemaphoreType.DMA((line, plane)),
        ],
        compiler_params=pltpu.CompilerParams(
            collective_id=0, has_side_effects=True, vmem_limit_bytes=VMEM_BYTES
        ),
        name="fetch",
    )(wanted, scales, dens, collocation, coords, weights[:, None, :])


def return_kernel(
    plane, line, tables_ref, outgoing_ref, prev_ref, out_ref, *scratch
):
    received, rest = scratch[:line], scratch[line:]
    running, part, inbox, hop_send, hop_recv, local_sem, send_sem, recv_sem = rest
    capacity = outgoing_ref.shape[1]
    stored, width, _ = prev_ref.shape
    entries = plane * capacity
    me = lax.axis_index("grid")
    z, q = me // plane, lax.rem(me, plane)
    order = [jnp.where(z == 0, line - 1 - p, jnp.where(z == line - 1, (p + 1) % line, (2, 1, 3, 0)[p])) for p in range(line)]
    greet(z, q, plane, line)

    def to_mate(p, k):
        to = lax.rem(q + k, plane)
        return pltpu.make_async_remote_copy(
            src_ref=outgoing_ref.at[lax.rem(z + order[p], line) * plane + to],
            dst_ref=received[p].at[pl.ds(q * capacity, capacity)],
            send_sem=send_sem.at[p, k],
            recv_sem=recv_sem.at[p, k],
            device_id=mate(z, to, plane),
            device_id_type=pl.DeviceIdType.MESH,
        )

    def to_self(p):
        return pltpu.make_async_copy(
            outgoing_ref.at[lax.rem(z + order[p], line) * plane + q],
            received[p].at[pl.ds(q * capacity, capacity)],
            local_sem.at[p],
        )

    def exchange(p):
        def one(k, carry):
            to_mate(p, k).start()
            return carry

        lax.fori_loop(1, plane, one, 0)
        to_self(p).start()

    def hop(p, up):
        to = order[p] - 1 if up else order[p] + 1
        return pltpu.make_async_remote_copy(
            src_ref=part.at[p],
            dst_ref=inbox.at[to],
            send_sem=hop_send.at[p],
            recv_sem=hop_recv.at[to],
            device_id=mate(z + 1 if up else z - 1, q, plane),
            device_id_type=pl.DeviceIdType.MESH,
        )

    def arrival(slot):
        return pltpu.make_async_remote_copy(
            src_ref=part.at[0],
            dst_ref=inbox.at[slot],
            send_sem=hop_send.at[0],
            recv_sem=hop_recv.at[slot],
            device_id=mate(z, lax.rem(q + 1, plane), plane),
            device_id_type=pl.DeviceIdType.MESH,
        )

    def gather(p):
        def finish(k, carry):
            to_mate(p, k).wait()
            return carry

        lax.fori_loop(1, plane, finish, 0)
        to_self(p).wait()
        if p + 2 < line:
            exchange(p + 2)
        row = lax.rem(z + order[p], line)

        def one(k, total):
            tile = received[p][tables_ref[row, 0, k]].astype(jnp.float32)
            total = jnp.where(tables_ref[row, 1, k] != 0, total, 0.0) + tile
            running[k] = total
            return total

        lax.fori_loop(0, entries, one, jnp.zeros((width, width), jnp.float32))

    def slot_sum(p, t):
        row = lax.rem(z + order[p], line)
        return jnp.where(tables_ref[row, 3, t] != 0, running[tables_ref[row, 2, t]], 0.0)

    def each(body):
        def one(t, carry):
            body(t)
            return carry

        lax.fori_loop(0, stored, one, 0)

    exchange(0)
    exchange(1)
    for p in range(line - 1):
        gather(p)
        up = z + order[p] < line
        feeds = jnp.where(up, z > 0, z < line - 1)

        @pl.when(feeds)
        def _():
            arrival(order[p]).wait_recv()

            def body(t):
                part[p, t] = (slot_sum(p, t) + inbox[order[p], t].astype(jnp.float32)).astype(jnp.bfloat16)

            each(body)

        @pl.when(jnp.logical_not(feeds))
        def _():
            def body(t):
                part[p, t] = slot_sum(p, t).astype(jnp.bfloat16)

            each(body)

        pl.when(up)(lambda: hop(p, True).start())
        pl.when(jnp.logical_not(up))(lambda: hop(p, False).start())
    gather(line - 1)

    def first(t):
        out_ref[t] = prev_ref[t].astype(jnp.float32) - 0.5 * slot_sum(line - 1, t)

    each(first)
    for slot, there in ((0, z > 0), (line, z < line - 1)):

        @pl.when(there)
        def _():
            arrival(slot).wait_recv()

            def body(t):
                out_ref[t] = out_ref[t] - 0.5 * inbox[slot, t].astype(jnp.float32)

            each(body)

    for p in range(line - 1):
        arrival_of = pltpu.make_async_remote_copy(
            src_ref=part.at[p],
            dst_ref=inbox.at[0],
            send_sem=hop_send.at[p],
            recv_sem=hop_recv.at[0],
            device_id=mate(z, lax.rem(q + 1, plane), plane),
            device_id_type=pl.DeviceIdType.MESH,
        )
        arrival_of.wait_send()


def give_back(tables, outgoing, prev, plane, line):
    stored, width, _ = prev.shape
    capacity = outgoing.shape[1]
    vmem, smem = pl.BlockSpec(memory_space=pltpu.VMEM), pl.BlockSpec(memory_space=pltpu.SMEM)
    return pl.pallas_call(
        functools.partial(return_kernel, plane, line),
        out_shape=jax.ShapeDtypeStruct((stored, width, width), jnp.float32),
        in_specs=[smem, pl.BlockSpec(memory_space=pl.ANY), vmem],
        out_specs=vmem,
        scratch_shapes=[pltpu.VMEM((plane * capacity, width, width), jnp.bfloat16)] * line
        + [
            pltpu.VMEM((plane * capacity, width, width), jnp.float32),
            pltpu.VMEM((line - 1, stored, width, width), jnp.bfloat16),
            pltpu.VMEM((line + 1, stored, width, width), jnp.bfloat16),
            pltpu.SemaphoreType.DMA((line - 1,)),
            pltpu.SemaphoreType.DMA((line + 1,)),
            pltpu.SemaphoreType.DMA((line,)),
            pltpu.SemaphoreType.DMA((line, plane)),
            pltpu.SemaphoreType.DMA((line, plane)),
        ],
        compiler_params=pltpu.CompilerParams(
            collective_id=1, has_side_effects=True, vmem_limit_bytes=VMEM_BYTES
        ),
        name="give_back",
    )(tables, outgoing, prev)


def shards(collocation, coords, weights, owners, slots, counts, dens_tiles, dens_scales, fock_prev):
    npeer = lax.axis_size("grid")
    per_dev, npair = owners.shape
    width = dens_tiles.shape[1]
    entries = per_dev * npair
    capacity = entries // npeer
    flat_owner = owners.reshape(-1)
    flat_slot = slots.reshape(-1)
    onehot = (flat_owner[:, None] == jnp.arange(npeer, dtype=jnp.int32)[None, :]).astype(jnp.bfloat16)
    before = jnp.tril(jnp.ones((entries, entries), jnp.bfloat16), -1)
    running = jnp.dot(before, onehot, preferred_element_type=jnp.float32)
    rank = jnp.sum(running * onehot.astype(jnp.float32), axis=1).astype(jnp.int32)
    pos = flat_owner * capacity + rank
    ranked = jnp.where(
        rank[:, None] == jnp.arange(capacity, dtype=jnp.int32)[None, :], flat_slot[:, None], 0
    )
    requests = jnp.dot(
        onehot.T, ranked.astype(jnp.bfloat16), preferred_element_type=jnp.float32
    ).astype(jnp.int32)
    plane = 8
    line = npeer // plane
    if line == 4 and plane * capacity >= dens_tiles.shape[0]:
        wanted = requests.reshape(line, plane, capacity).transpose(1, 0, 2).reshape(plane, 1, line * capacity)
        wanted = jnp.pad(wanted, ((0, 0), (0, 7), (0, 128 - line * capacity)))
        fetched, metric, tables = fetch(
            wanted, dens_scales, dens_tiles, collocation, coords, weights, plane, line, capacity
        )
        outgoing = apply_metric(pos, counts, fetched.reshape(entries, width, width), metric)
        return give_back(tables, outgoing.reshape(npeer, capacity, width, width), fock_prev, plane, line)
    asked = lax.all_to_all(requests, "grid", split_axis=0, concat_axis=0, tiled=True).reshape(-1)
    chunk = 16
    tiles = pick(asked, dens_scales, dens_tiles, chunk)
    metric = metric_of(collocation, coords, weights)
    fetched = lax.all_to_all(
        tiles.reshape(npeer, capacity, width, width), "grid", split_axis=0, concat_axis=0, tiled=True
    ).reshape(entries, width, width)
    outgoing = apply_metric(pos, counts, fetched, metric)
    received = lax.all_to_all(
        outgoing.reshape(npeer, capacity, width, width), "grid", split_axis=0, concat_axis=0, tiled=True
    ).reshape(entries, width, width)
    return update(asked, received, fock_prev, chunk)


def solution(mesh):
    split = ("groups", "grid")
    return jax.shard_map(
        shards,
        mesh=mesh,
        in_specs=(
            P(split, None, None),
            P(split, None, None),
            P(split, None),
            P(split, None),
            P(split, None),
            P(split),
            P(split, None, None),
            P(split),
            P(split, None, None),
        ),
        out_specs=P(split, None, None),
        check_vma=False,
    )
```

```python
import functools

import jax
import jax.numpy as jnp
from jax import lax
from jax.experimental import pallas as pl
from jax.experimental.pallas import tpu as pltpu
from jax.sharding import PartitionSpec as P

SOFTEN = 0.5
VMEM_BYTES = 56 * 2**20


def metric_kernel(colloc_ref, coords_ref, weights_ref, metric_ref):
    points = colloc_ref.shape[0]
    xyz = coords_ref[...]
    w = weights_ref[...]
    rows = jnp.concatenate([xyz, w, jnp.zeros((4, points), jnp.float32)], axis=0)
    cols = rows.T
    a = colloc_ref[...]
    total = jnp.full((points, points), SOFTEN * SOFTEN, jnp.float32)
    for axis in range(3):
        diff = cols[:, axis : axis + 1] - xyz[axis : axis + 1, :]
        total = total + diff * diff
    kern = (cols[:, 3:4] * w * lax.rsqrt(total)).astype(jnp.bfloat16)
    smeared = jnp.dot(kern, a, preferred_element_type=jnp.float32).astype(jnp.bfloat16)
    metric_ref[...] = lax.dot_general(
        a, smeared, (((0,), (0,)), ((), ())), preferred_element_type=jnp.float32
    ).astype(jnp.bfloat16)


def metric_of(collocation, coords, weights):
    per_dev, points, funcs = collocation.shape
    return pl.pallas_call(
        metric_kernel,
        grid=(per_dev,),
        out_shape=jax.ShapeDtypeStruct((per_dev, funcs, funcs), jnp.bfloat16),
        in_specs=[
            pl.BlockSpec((None, points, funcs), lambda b: (b, 0, 0)),
            pl.BlockSpec((None, 3, points), lambda b: (b, 0, 0)),
            pl.BlockSpec((None, 1, points), lambda b: (b, 0, 0)),
        ],
        out_specs=pl.BlockSpec((None, funcs, funcs), lambda b: (b, 0, 0)),
        compiler_params=pltpu.CompilerParams(vmem_limit_bytes=VMEM_BYTES),
        cost_estimate=pl.CostEstimate(
            flops=4 * per_dev * points * points * funcs,
            bytes_accessed=4 * per_dev * points * funcs,
            transcendentals=per_dev * points * points,
        ),
        name="metric",
    )(collocation, coords, weights[:, None, :])


def pick_kernel(asked_ref, scales_ref, dens_ref, out_ref, scaled):
    stored = dens_ref.shape[0]
    count = out_ref.shape[0]
    step = pl.program_id(0)

    @pl.when(step == 0)
    def _():
        def one(t, carry):
            scaled[t] = (dens_ref[t].astype(jnp.float32) * scales_ref[t]).astype(jnp.bfloat16)
            return carry

        lax.fori_loop(0, stored, one, 0)

    for k in range(count):
        out_ref[k] = scaled[asked_ref[step * count + k]]


def pick(asked, scales, dens, chunk):
    total = asked.shape[0]
    stored, width, _ = dens.shape
    return pl.pallas_call(
        pick_kernel,
        out_shape=jax.ShapeDtypeStruct((total, width, width), jnp.bfloat16),
        grid_spec=pltpu.PrefetchScalarGridSpec(
            num_scalar_prefetch=2,
            grid=(total // chunk,),
            in_specs=[pl.BlockSpec((stored, width, width), lambda s, *_: (0, 0, 0))],
            out_specs=pl.BlockSpec((chunk, width, width), lambda s, *_: (s, 0, 0)),
            scratch_shapes=[pltpu.VMEM((stored, width, width), jnp.bfloat16)],
        ),
        compiler_params=pltpu.CompilerParams(vmem_limit_bytes=VMEM_BYTES),
        name="pick",
    )(asked, scales, dens)


def apply_kernel(listed, pos_ref, counts_ref, fetched_ref, metric_ref, out_ref, dmat):
    width = fetched_ref.shape[1]
    b = pl.program_id(0)
    count = jnp.clip(counts_ref[b], 0, listed)

    def at(i, j):
        return pos_ref[b * listed * listed + i * listed + j]

    def live(size):
        for i in range(size):
            for j in range(size):
                dmat[i * width : (i + 1) * width, j * width : (j + 1) * width] = fetched_ref[at(i, j)]
        span = size * width
        for i in range(size):
            parts = jnp.dot(
                metric_ref[i * width : (i + 1) * width, :span], dmat[:span, :span], preferred_element_type=jnp.float32
            ).astype(jnp.bfloat16)
            for j in range(size):
                out_ref[at(i, j)] = parts[:, j * width : (j + 1) * width]

    def branch(size):
        if size:
            live(size)
        for i in range(listed):
            for j in range(listed):
                if max(i, j) >= size:
                    out_ref[at(i, j)] = jnp.zeros((width, width), jnp.bfloat16)

    for size in range(listed + 1):
        pl.when(count == size)(functools.partial(branch, size))


def apply_metric(pos, counts, fetched, metric):
    total, width, _ = fetched.shape
    per_dev, funcs, _ = metric.shape
    return pl.pallas_call(
        functools.partial(apply_kernel, funcs // width),
        out_shape=jax.ShapeDtypeStruct((total, width, width), jnp.bfloat16),
        grid_spec=pltpu.PrefetchScalarGridSpec(
            num_scalar_prefetch=2,
            grid=(per_dev,),
            in_specs=[
                pl.BlockSpec(
                    (total, width, width), lambda b, *_: (0, 0, 0), pipeline_mode=pl.Buffered(1)
                ),
                pl.BlockSpec((None, funcs, funcs), lambda b, *_: (b, 0, 0)),
            ],
            out_specs=pl.BlockSpec((total, width, width), lambda b, *_: (0, 0, 0)),
            scratch_shapes=[pltpu.VMEM((funcs, funcs), jnp.bfloat16)],
        ),
        compiler_params=pltpu.CompilerParams(vmem_limit_bytes=VMEM_BYTES),
        name="apply_metric",
    )(pos, counts, fetched, metric)


def update_kernel(asked_ref, received_ref, prev_ref, out_ref):
    count = received_ref.shape[0]
    step = pl.program_id(0)

    @pl.when(step == 0)
    def _():
        out_ref[...] = prev_ref[...].astype(jnp.float32)

    for k in range(count):
        slot = asked_ref[step * count + k]
        out_ref[slot] = out_ref[slot] - 0.5 * received_ref[k].astype(jnp.float32)


def update(asked, received, prev, chunk):
    total, width, _ = received.shape
    stored = prev.shape[0]
    return pl.pallas_call(
        update_kernel,
        out_shape=jax.ShapeDtypeStruct((stored, width, width), jnp.float32),
        grid_spec=pltpu.PrefetchScalarGridSpec(
            num_scalar_prefetch=1,
            grid=(total // chunk,),
            in_specs=[
                pl.BlockSpec((chunk, width, width), lambda s, *_: (s, 0, 0)),
                pl.BlockSpec((stored, width, width), lambda s, *_: (0, 0, 0)),
            ],
            out_specs=pl.BlockSpec((stored, width, width), lambda s, *_: (0, 0, 0)),
        ),
        compiler_params=pltpu.CompilerParams(vmem_limit_bytes=VMEM_BYTES),
        name="update",
    )(asked, received, prev)


def mate(z, lane, plane):
    return {"grid": z * plane + lane}


def greet(z, q, plane, line):
    barrier = pltpu.get_barrier_semaphore()
    for k in range(1, plane):
        pl.semaphore_signal(
            barrier, inc=1, device_id=mate(z, lax.rem(q + k, plane), plane), device_id_type=pl.DeviceIdType.MESH
        )

    @pl.when(z > 0)
    def _():
        pl.semaphore_signal(barrier, inc=1, device_id=mate(z - 1, q, plane), device_id_type=pl.DeviceIdType.MESH)

    @pl.when(z < line - 1)
    def _():
        pl.semaphore_signal(barrier, inc=1, device_id=mate(z + 1, q, plane), device_id_type=pl.DeviceIdType.MESH)

    pl.semaphore_wait(barrier, plane - 1 + jnp.where(z > 0, 1, 0) + jnp.where(z < line - 1, 1, 0))


def slot_tables(asked_ref, tables_ref, line, capacity):
    entries = tables_ref.shape[2]
    row = lax.broadcasted_iota(jnp.int32, (entries, entries), 0)
    column = lax.broadcasted_iota(jnp.int32, (entries, entries), 1)

    def ones(mask):
        return jnp.where(mask, 1.0, 0.0)

    for source in range(line):

        def spread(e, carry):
            down, across = carry
            slot = asked_ref[e // capacity, 0, source * capacity + e % capacity]
            return jnp.where(row == e, slot, down), jnp.where(column == e, slot, across)

        zero = jnp.zeros((entries, entries), jnp.int32)
        mine, other = lax.fori_loop(0, entries, spread, (zero, zero))
        twin = (other == mine) & (column < row)
        place = jnp.sum(ones((other < mine) | twin), axis=1, keepdims=True)
        shared = jnp.max(ones(twin), axis=1, keepdims=True)
        at = place == column.astype(jnp.float32)
        tables_ref[source, 0:1, :] = jnp.sum(jnp.where(at, row.astype(jnp.float32), 0.0), axis=0, keepdims=True).astype(jnp.int32)
        tables_ref[source, 1:2, :] = jnp.sum(jnp.where(at, shared, 0.0), axis=0, keepdims=True).astype(jnp.int32)
        upto = jnp.sum(ones(mine <= column), axis=0, keepdims=True)
        tables_ref[source, 2:3, :] = jnp.maximum(upto - 1.0, 0.0).astype(jnp.int32)
        tables_ref[source, 3:4, :] = jnp.max(ones(mine == column), axis=0, keepdims=True).astype(jnp.int32)
        tables_ref[source, 4:8, :] = jnp.zeros((4, entries), jnp.int32)


def fetch_kernel(
    plane, line, wanted_ref, scales_ref, pos_ref, inverse_ref, counts_ref, dens_ref, colloc_hbm, coords_ref,
    weights_ref, outgoing_ref, tables_ref, *scratch
):
    pools, rest = scratch[:line], scratch[line:]
    stage, fetched_ref, parts_ref, dmat_ref, colloc_ref, metric_ref, asked_vmem, asked_ref = rest[:8]
    in_sem, out_sem, smem_sem, ask_send, ask_recv, hop_send, hop_recv, local_sem, send_sem, recv_sem = rest[8:]
    capacity, width = stage.shape[2:4]
    listed = colloc_ref.shape[2] // width
    stored = dens_ref.shape[0]
    batches = colloc_ref.shape[0]
    me = lax.axis_index("grid")
    z, q = me // plane, lax.rem(me, plane)
    load = pltpu.make_async_copy(colloc_hbm, colloc_ref, in_sem)
    load.start()

    def scale(t, carry):
        pools[0][t] = (dens_ref[t].astype(jnp.float32) * scales_ref[t]).astype(jnp.bfloat16)
        return carry

    lax.fori_loop(0, stored, scale, 0)
    greet(z, q, plane, line)

    def hop(slot, up):
        to_slot = (slot + 1 if up else slot - 1) % line
        return pltpu.make_async_remote_copy(
            src_ref=pools[slot],
            dst_ref=pools[to_slot],
            send_sem=hop_send.at[line if (slot == 0 and not up) else slot],
            recv_sem=hop_recv.at[to_slot],
            device_id=mate(z + 1 if up else z - 1, q, plane),
            device_id_type=pl.DeviceIdType.MESH,
        )

    def hops(slot, act):
        if slot + 1 < line:

            @pl.when((z >= slot) & (z < line - 1))
            def _():
                act(hop(slot, True))

        if slot != 1:

            @pl.when(((z < slot) | (slot == 0)) & (z > 0))
            def _():
                act(hop(slot, False))

    def to_mate(slot, k):
        owner = lax.rem(z - slot + line, line) * plane + q
        return pltpu.make_async_remote_copy(
            src_ref=stage.at[slot, k],
            dst_ref=fetched_ref.at[pl.ds(owner * capacity, capacity)],
            send_sem=send_sem.at[slot, k],
            recv_sem=recv_sem.at[slot, k],
            device_id=mate(z, lax.rem(q + k, plane), plane),
            device_id_type=pl.DeviceIdType.MESH,
        )

    def to_self(slot):
        owner = lax.rem(z - slot + line, line) * plane + q
        return pltpu.make_async_copy(
            stage.at[slot, 0], fetched_ref.at[pl.ds(owner * capacity, capacity)], local_sem.at[slot]
        )

    def serve(slot):
        if slot:
            hop(slot - 1, True).wait_recv()
            hops(slot, lambda copy: copy.start())
        source = lax.rem(z - slot + line, line)

        def fill(k):
            to = lax.rem(q + k, plane)
            for r in range(capacity):
                stage[slot, k, r] = pools[slot][asked_ref[to, 0, source * capacity + r]]

        def one(k, carry):
            fill(k)
            to_mate(slot, k).start()
            return carry

        lax.fori_loop(1, plane, one, 0)
        fill(0)
        to_self(slot).start()

    def metrics(first, last):
        def one(b, carry):
            metric_kernel(colloc_ref.at[b], coords_ref.at[b], weights_ref.at[pl.ds(b, 1)], metric_ref.at[b])
            return carry

        lax.fori_loop(first, last, one, 0)

    def ask(k):
        return pltpu.make_async_remote_copy(
            src_ref=wanted_ref.at[lax.rem(q + k, plane)],
            dst_ref=asked_vmem.at[q],
            send_sem=ask_send.at[k],
            recv_sem=ask_recv.at[k],
            device_id=mate(z, lax.rem(q + k, plane), plane),
            device_id_type=pl.DeviceIdType.MESH,
        )

    for k in range(1, plane):
        ask(k).start()
    own = pltpu.make_async_copy(wanted_ref.at[q], asked_vmem.at[q], ask_send.at[0])
    own.start()
    hops(0, lambda copy: copy.start())
    own.wait()
    for k in range(1, plane):
        ask(k).wait()
    scalars = pltpu.make_async_copy(asked_vmem, asked_ref, smem_sem)
    scalars.start()
    scalars.wait()
    serve(0)
    slot_tables(asked_ref, tables_ref, line, capacity)
    load.wait()
    for d in range(1, line):
        metrics(batches * (d - 1) // (line - 1), batches * d // (line - 1))
        if 2 * d == line:
            serve(d)
        else:
            pl.when(z >= d)(functools.partial(serve, d))
            pl.when(z + d < line)(functools.partial(serve, line - d))
    for slot in range(line):
        hops(slot, lambda copy: copy.wait_send())
        to_self(slot).wait()

        def finish(k, carry):
            to_mate(slot, k).wait()
            return carry

        lax.fori_loop(1, plane, finish, 0)

    def product(b, buffer):
        count = counts_ref[b]
        for i in range(listed):
            for j in range(listed):
                tile = fetched_ref[pos_ref[(b * listed + i) * listed + j]]
                dmat_ref[buffer, i * width : (i + 1) * width, j * width : (j + 1) * width] = jnp.where(
                    max(i, j) < count, tile, jnp.zeros_like(tile)
                )
        parts = jnp.dot(metric_ref[b], dmat_ref[buffer], preferred_element_type=jnp.float32)
        for i in range(listed):
            for j in range(listed):
                part = parts[i * width : (i + 1) * width, j * width : (j + 1) * width].astype(jnp.bfloat16)
                parts_ref[(b * listed + i) * listed + j] = jnp.where(max(i, j) < count, part, jnp.zeros_like(part))

    buffers = dmat_ref.shape[0]

    def products(step, carry):
        for buffer in range(buffers):
            product(step * buffers + buffer, buffer)
        return carry

    lax.fori_loop(0, batches // buffers, products, 0)

    def put_out(source):
        return pltpu.make_async_copy(
            stage.at[source], outgoing_ref.at[pl.ds(source * plane, plane)], out_sem.at[source]
        )

    for source in range(line):

        def arrange(lane, carry):
            for r in range(capacity):
                stage[source, lane, r] = parts_ref[inverse_ref[(source * plane + lane) * capacity + r]]
            return carry

        lax.fori_loop(0, plane, arrange, 0)
        put_out(source).start()
    for source in range(line):
        put_out(source).wait()


def fetch(wanted, scales, pos, inverse, counts, dens, collocation, coords, weights, plane, line, capacity):
    stored, width, _ = dens.shape
    per_dev, points, funcs = collocation.shape
    vmem, smem = pl.BlockSpec(memory_space=pltpu.VMEM), pl.BlockSpec(memory_space=pltpu.SMEM)
    hbm = pl.BlockSpec(memory_space=pl.ANY)
    return pl.pallas_call(
        functools.partial(fetch_kernel, plane, line),
        out_shape=(
            jax.ShapeDtypeStruct((line * plane, capacity, width, width), jnp.bfloat16),
            jax.ShapeDtypeStruct((line, 8, plane * capacity), jnp.int32),
        ),
        in_specs=[vmem, smem, smem, smem, smem, vmem, hbm, vmem, vmem],
        out_specs=(hbm, vmem),
        scratch_shapes=[pltpu.VMEM((stored, width, width), jnp.bfloat16)] * line
        + [
            pltpu.VMEM((line, plane, capacity, width, width), jnp.bfloat16),
            pltpu.VMEM((line * plane * capacity, width, width), jnp.bfloat16),
            pltpu.VMEM((line * plane * capacity, width, width), jnp.bfloat16),
            pltpu.VMEM((2 - per_dev % 2, funcs, funcs), jnp.bfloat16),
            pltpu.VMEM((per_dev, points, funcs), jnp.bfloat16),
            pltpu.VMEM((per_dev, funcs, funcs), jnp.bfloat16),
            pltpu.VMEM(wanted.shape, jnp.int32),
            pltpu.SMEM(wanted.shape, jnp.int32),
            pltpu.SemaphoreType.DMA,
            pltpu.SemaphoreType.DMA((line,)),
            pltpu.SemaphoreType.DMA,
            pltpu.SemaphoreType.DMA((plane,)),
            pltpu.SemaphoreType.DMA((plane,)),
            pltpu.SemaphoreType.DMA((line + 1,)),
            pltpu.SemaphoreType.DMA((line,)),
            pltpu.SemaphoreType.DMA((line,)),
            pltpu.SemaphoreType.DMA((line, plane)),
            pltpu.SemaphoreType.DMA((line, plane)),
        ],
        compiler_params=pltpu.CompilerParams(
            collective_id=0, has_side_effects=True, vmem_limit_bytes=VMEM_BYTES
        ),
        name="fetch",
    )(wanted, scales, pos, inverse, counts, dens, collocation, coords, weights)


def return_kernel(
    plane, line, tables_ref, outgoing_ref, prev_ref, out_ref, *scratch
):
    received, rest = scratch[:line], scratch[line:]
    running, part, inbox, hop_send, hop_recv, local_sem, send_sem, recv_sem = rest
    capacity = outgoing_ref.shape[1]
    stored, width, _ = prev_ref.shape
    entries = plane * capacity
    me = lax.axis_index("grid")
    z, q = me // plane, lax.rem(me, plane)
    order = [jnp.where(z == 0, line - 1 - p, jnp.where(z == line - 1, (p + 1) % line, (2, 1, 3, 0)[p])) for p in range(line)]
    greet(z, q, plane, line)

    def to_mate(p, k):
        to = lax.rem(q + k, plane)
        return pltpu.make_async_remote_copy(
            src_ref=outgoing_ref.at[lax.rem(z + order[p], line) * plane + to],
            dst_ref=received[p].at[pl.ds(q * capacity, capacity)],
            send_sem=send_sem.at[p, k],
            recv_sem=recv_sem.at[p, k],
            device_id=mate(z, to, plane),
            device_id_type=pl.DeviceIdType.MESH,
        )

    def to_self(p):
        return pltpu.make_async_copy(
            outgoing_ref.at[lax.rem(z + order[p], line) * plane + q],
            received[p].at[pl.ds(q * capacity, capacity)],
            local_sem.at[p],
        )

    def exchange(p):
        def one(k, carry):
            to_mate(p, k).start()
            return carry

        lax.fori_loop(1, plane, one, 0)
        to_self(p).start()

    def hop(p, up):
        to = order[p] - 1 if up else order[p] + 1
        return pltpu.make_async_remote_copy(
            src_ref=part.at[p],
            dst_ref=inbox.at[to],
            send_sem=hop_send.at[p],
            recv_sem=hop_recv.at[to],
            device_id=mate(z + 1 if up else z - 1, q, plane),
            device_id_type=pl.DeviceIdType.MESH,
        )

    def arrival(slot):
        return pltpu.make_async_remote_copy(
            src_ref=part.at[0],
            dst_ref=inbox.at[slot],
            send_sem=hop_send.at[0],
            recv_sem=hop_recv.at[slot],
            device_id=mate(z, lax.rem(q + 1, plane), plane),
            device_id_type=pl.DeviceIdType.MESH,
        )

    def gather(p):
        def finish(k, carry):
            to_mate(p, k).wait()
            return carry

        lax.fori_loop(1, plane, finish, 0)
        to_self(p).wait()
        if p + 2 < line:
            exchange(p + 2)
        row = lax.rem(z + order[p], line)

        def one(k, total):
            tile = received[p][tables_ref[row, 0, k]].astype(jnp.float32)
            total = jnp.where(tables_ref[row, 1, k] != 0, total, 0.0) + tile
            running[k] = total
            return total

        lax.fori_loop(0, entries, one, jnp.zeros((width, width), jnp.float32), unroll=4)

    def slot_sum(p, t):
        row = lax.rem(z + order[p], line)
        return jnp.where(tables_ref[row, 3, t] != 0, running[tables_ref[row, 2, t]], 0.0)

    def each(body):
        def one(t, carry):
            body(t)
            return carry

        lax.fori_loop(0, stored, one, 0, unroll=4)

    exchange(0)
    exchange(1)
    for p in range(line - 1):
        gather(p)
        up = z + order[p] < line
        feeds = jnp.where(up, z > 0, z < line - 1)

        @pl.when(feeds)
        def _():
            arrival(order[p]).wait_recv()

            def body(t):
                part[p, t] = (slot_sum(p, t) + inbox[order[p], t].astype(jnp.float32)).astype(jnp.bfloat16)

            each(body)

        @pl.when(jnp.logical_not(feeds))
        def _():
            def body(t):
                part[p, t] = slot_sum(p, t).astype(jnp.bfloat16)

            each(body)

        pl.when(up)(lambda: hop(p, True).start())
        pl.when(jnp.logical_not(up))(lambda: hop(p, False).start())
    gather(line - 1)

    def first(t):
        out_ref[t] = prev_ref[t].astype(jnp.float32) - 0.5 * slot_sum(line - 1, t)

    each(first)
    for slot, there in ((0, z > 0), (line, z < line - 1)):

        @pl.when(there)
        def _():
            arrival(slot).wait_recv()

            def body(t):
                out_ref[t] = out_ref[t] - 0.5 * inbox[slot, t].astype(jnp.float32)

            each(body)

    for p in range(line - 1):
        arrival_of = pltpu.make_async_remote_copy(
            src_ref=part.at[p],
            dst_ref=inbox.at[0],
            send_sem=hop_send.at[p],
            recv_sem=hop_recv.at[0],
            device_id=mate(z, lax.rem(q + 1, plane), plane),
            device_id_type=pl.DeviceIdType.MESH,
        )
        arrival_of.wait_send()


def give_back(tables, outgoing, prev, plane, line):
    stored, width, _ = prev.shape
    capacity = outgoing.shape[1]
    vmem, smem = pl.BlockSpec(memory_space=pltpu.VMEM), pl.BlockSpec(memory_space=pltpu.SMEM)
    return pl.pallas_call(
        functools.partial(return_kernel, plane, line),
        out_shape=jax.ShapeDtypeStruct((stored, width, width), jnp.float32),
        in_specs=[smem, pl.BlockSpec(memory_space=pl.ANY), vmem],
        out_specs=vmem,
        scratch_shapes=[pltpu.VMEM((plane * capacity, width, width), jnp.bfloat16)] * line
        + [
            pltpu.VMEM((plane * capacity, width, width), jnp.float32),
            pltpu.VMEM((line - 1, stored, width, width), jnp.bfloat16),
            pltpu.VMEM((line + 1, stored, width, width), jnp.bfloat16),
            pltpu.SemaphoreType.DMA((line - 1,)),
            pltpu.SemaphoreType.DMA((line + 1,)),
            pltpu.SemaphoreType.DMA((line,)),
            pltpu.SemaphoreType.DMA((line, plane)),
            pltpu.SemaphoreType.DMA((line, plane)),
        ],
        compiler_params=pltpu.CompilerParams(
            collective_id=1, has_side_effects=True, vmem_limit_bytes=VMEM_BYTES
        ),
        name="give_back",
    )(tables, outgoing, prev)


def shards(collocation, coords, weights, owners, slots, counts, dens_tiles, dens_scales, fock_prev):
    npeer = lax.axis_size("grid")
    per_dev, npair = owners.shape
    width = dens_tiles.shape[1]
    entries = per_dev * npair
    capacity = entries // npeer
    flat_owner = owners.reshape(-1)
    flat_slot = slots.reshape(-1)
    onehot = (flat_owner[:, None] == jnp.arange(npeer, dtype=jnp.int32)[None, :]).astype(jnp.bfloat16)
    before = jnp.tril(jnp.ones((entries, entries), jnp.bfloat16), -1)
    running = jnp.dot(before, onehot, preferred_element_type=jnp.float32)
    rank = jnp.sum(running * onehot.astype(jnp.float32), axis=1).astype(jnp.int32)
    pos = flat_owner * capacity + rank
    ranked = jnp.where(
        rank[:, None] == jnp.arange(capacity, dtype=jnp.int32)[None, :], flat_slot[:, None], 0
    )
    requests = jnp.dot(
        onehot.T, ranked.astype(jnp.bfloat16), preferred_element_type=jnp.float32
    ).astype(jnp.int32)
    plane = 8
    line = npeer // plane
    if line == 4 and plane * capacity >= dens_tiles.shape[0]:
        wanted = requests.reshape(line, plane, capacity).transpose(1, 0, 2).reshape(plane, 1, line * capacity)
        wanted = jnp.pad(wanted, ((0, 0), (0, 7), (0, 128 - line * capacity)))
        index = jnp.arange(entries, dtype=jnp.int32)[:, None]
        numbered = jnp.where(rank[:, None] == jnp.arange(capacity, dtype=jnp.int32)[None, :], index, 0)
        inverse = jnp.dot(
            onehot.T.astype(jnp.float32), numbered.astype(jnp.float32), precision=lax.Precision.HIGHEST
        ).astype(jnp.int32)
        outgoing, tables = fetch(
            wanted, dens_scales, pos, inverse.reshape(-1), counts, dens_tiles, collocation, coords, weights,
            plane, line, capacity,
        )
        return give_back(tables, outgoing, fock_prev, plane, line)
    asked = lax.all_to_all(requests, "grid", split_axis=0, concat_axis=0, tiled=True).reshape(-1)
    chunk = 16
    tiles = pick(asked, dens_scales, dens_tiles, chunk)
    metric = metric_of(collocation, coords, weights)
    fetched = lax.all_to_all(
        tiles.reshape(npeer, capacity, width, width), "grid", split_axis=0, concat_axis=0, tiled=True
    ).reshape(entries, width, width)
    outgoing = apply_metric(pos, counts, fetched, metric)
    received = lax.all_to_all(
        outgoing.reshape(npeer, capacity, width, width), "grid", split_axis=0, concat_axis=0, tiled=True
    ).reshape(entries, width, width)
    return update(asked, received, fock_prev, chunk)


def solution(mesh):
    split = ("groups", "grid")
    return jax.shard_map(
        shards,
        mesh=mesh,
        in_specs=(
            P(split, None, None),
            P(split, None, None),
            P(split, None),
            P(split, None),
            P(split, None),
            P(split),
            P(split, None, None),
            P(split),
            P(split, None, None),
        ),
        out_specs=P(split, None, None),
        check_vma=False,
    )
```

```python
import functools

import jax
import jax.numpy as jnp
from jax import lax
from jax.experimental import pallas as pl
from jax.experimental.pallas import tpu as pltpu
from jax.sharding import PartitionSpec as P

SOFTEN = 0.5
VMEM_BYTES = 62 * 2**20


def metric_kernel(colloc_ref, coords_ref, weights_ref, metric_ref):
    points = colloc_ref.shape[0]
    xyz = coords_ref[...]
    w = weights_ref[...]
    rows = jnp.concatenate([xyz, w, jnp.zeros((4, points), jnp.float32)], axis=0)
    cols = rows.T
    a = colloc_ref[...]
    total = jnp.full((points, points), SOFTEN * SOFTEN, jnp.float32)
    for axis in range(3):
        diff = cols[:, axis : axis + 1] - xyz[axis : axis + 1, :]
        total = total + diff * diff
    kern = (cols[:, 3:4] * w * lax.rsqrt(total)).astype(jnp.bfloat16)
    smeared = jnp.dot(kern, a, preferred_element_type=jnp.float32).astype(jnp.bfloat16)
    metric_ref[...] = lax.dot_general(
        a, smeared, (((0,), (0,)), ((), ())), preferred_element_type=jnp.float32
    ).astype(jnp.bfloat16)


def metric_of(collocation, coords, weights):
    per_dev, points, funcs = collocation.shape
    return pl.pallas_call(
        metric_kernel,
        grid=(per_dev,),
        out_shape=jax.ShapeDtypeStruct((per_dev, funcs, funcs), jnp.bfloat16),
        in_specs=[
            pl.BlockSpec((None, points, funcs), lambda b: (b, 0, 0)),
            pl.BlockSpec((None, 3, points), lambda b: (b, 0, 0)),
            pl.BlockSpec((None, 1, points), lambda b: (b, 0, 0)),
        ],
        out_specs=pl.BlockSpec((None, funcs, funcs), lambda b: (b, 0, 0)),
        compiler_params=pltpu.CompilerParams(vmem_limit_bytes=VMEM_BYTES),
        cost_estimate=pl.CostEstimate(
            flops=4 * per_dev * points * points * funcs,
            bytes_accessed=4 * per_dev * points * funcs,
            transcendentals=per_dev * points * points,
        ),
        name="metric",
    )(collocation, coords, weights[:, None, :])


def pick_kernel(asked_ref, scales_ref, dens_ref, out_ref, scaled):
    stored = dens_ref.shape[0]
    count = out_ref.shape[0]
    step = pl.program_id(0)

    @pl.when(step == 0)
    def _():
        def one(t, carry):
            scaled[t] = (dens_ref[t].astype(jnp.float32) * scales_ref[t]).astype(jnp.bfloat16)
            return carry

        lax.fori_loop(0, stored, one, 0)

    for k in range(count):
        out_ref[k] = scaled[asked_ref[step * count + k]]


def pick(asked, scales, dens, chunk):
    total = asked.shape[0]
    stored, width, _ = dens.shape
    return pl.pallas_call(
        pick_kernel,
        out_shape=jax.ShapeDtypeStruct((total, width, width), jnp.bfloat16),
        grid_spec=pltpu.PrefetchScalarGridSpec(
            num_scalar_prefetch=2,
            grid=(total // chunk,),
            in_specs=[pl.BlockSpec((stored, width, width), lambda s, *_: (0, 0, 0))],
            out_specs=pl.BlockSpec((chunk, width, width), lambda s, *_: (s, 0, 0)),
            scratch_shapes=[pltpu.VMEM((stored, width, width), jnp.bfloat16)],
        ),
        compiler_params=pltpu.CompilerParams(vmem_limit_bytes=VMEM_BYTES),
        name="pick",
    )(asked, scales, dens)


def apply_kernel(listed, pos_ref, counts_ref, fetched_ref, metric_ref, out_ref, dmat):
    width = fetched_ref.shape[1]
    b = pl.program_id(0)
    count = jnp.clip(counts_ref[b], 0, listed)

    def at(i, j):
        return pos_ref[b * listed * listed + i * listed + j]

    def live(size):
        for i in range(size):
            for j in range(size):
                dmat[i * width : (i + 1) * width, j * width : (j + 1) * width] = fetched_ref[at(i, j)]
        span = size * width
        for i in range(size):
            parts = jnp.dot(
                metric_ref[i * width : (i + 1) * width, :span], dmat[:span, :span], preferred_element_type=jnp.float32
            ).astype(jnp.bfloat16)
            for j in range(size):
                out_ref[at(i, j)] = parts[:, j * width : (j + 1) * width]

    def branch(size):
        if size:
            live(size)
        for i in range(listed):
            for j in range(listed):
                if max(i, j) >= size:
                    out_ref[at(i, j)] = jnp.zeros((width, width), jnp.bfloat16)

    for size in range(listed + 1):
        pl.when(count == size)(functools.partial(branch, size))


def apply_metric(pos, counts, fetched, metric):
    total, width, _ = fetched.shape
    per_dev, funcs, _ = metric.shape
    return pl.pallas_call(
        functools.partial(apply_kernel, funcs // width),
        out_shape=jax.ShapeDtypeStruct((total, width, width), jnp.bfloat16),
        grid_spec=pltpu.PrefetchScalarGridSpec(
            num_scalar_prefetch=2,
            grid=(per_dev,),
            in_specs=[
                pl.BlockSpec(
                    (total, width, width), lambda b, *_: (0, 0, 0), pipeline_mode=pl.Buffered(1)
                ),
                pl.BlockSpec((None, funcs, funcs), lambda b, *_: (b, 0, 0)),
            ],
            out_specs=pl.BlockSpec((total, width, width), lambda b, *_: (0, 0, 0)),
            scratch_shapes=[pltpu.VMEM((funcs, funcs), jnp.bfloat16)],
        ),
        compiler_params=pltpu.CompilerParams(vmem_limit_bytes=VMEM_BYTES),
        name="apply_metric",
    )(pos, counts, fetched, metric)


def update_kernel(asked_ref, received_ref, prev_ref, out_ref):
    count = received_ref.shape[0]
    step = pl.program_id(0)

    @pl.when(step == 0)
    def _():
        out_ref[...] = prev_ref[...].astype(jnp.float32)

    for k in range(count):
        slot = asked_ref[step * count + k]
        out_ref[slot] = out_ref[slot] - 0.5 * received_ref[k].astype(jnp.float32)


def update(asked, received, prev, chunk):
    total, width, _ = received.shape
    stored = prev.shape[0]
    return pl.pallas_call(
        update_kernel,
        out_shape=jax.ShapeDtypeStruct((stored, width, width), jnp.float32),
        grid_spec=pltpu.PrefetchScalarGridSpec(
            num_scalar_prefetch=1,
            grid=(total // chunk,),
            in_specs=[
                pl.BlockSpec((chunk, width, width), lambda s, *_: (s, 0, 0)),
                pl.BlockSpec((stored, width, width), lambda s, *_: (0, 0, 0)),
            ],
            out_specs=pl.BlockSpec((stored, width, width), lambda s, *_: (0, 0, 0)),
        ),
        compiler_params=pltpu.CompilerParams(vmem_limit_bytes=VMEM_BYTES),
        name="update",
    )(asked, received, prev)


def mate(z, lane, plane):
    return {"grid": z * plane + lane}


def greet(z, q, plane, line):
    barrier = pltpu.get_barrier_semaphore()
    for k in range(1, plane):
        pl.semaphore_signal(
            barrier, inc=1, device_id=mate(z, lax.rem(q + k, plane), plane), device_id_type=pl.DeviceIdType.MESH
        )

    @pl.when(z > 0)
    def _():
        pl.semaphore_signal(barrier, inc=1, device_id=mate(z - 1, q, plane), device_id_type=pl.DeviceIdType.MESH)

    @pl.when(z < line - 1)
    def _():
        pl.semaphore_signal(barrier, inc=1, device_id=mate(z + 1, q, plane), device_id_type=pl.DeviceIdType.MESH)

    pl.semaphore_wait(barrier, plane - 1 + jnp.where(z > 0, 1, 0) + jnp.where(z < line - 1, 1, 0))


def slot_tables(asked_ref, tables_ref, line, capacity):
    entries = tables_ref.shape[2]
    row = lax.broadcasted_iota(jnp.int32, (entries, entries), 0)
    column = lax.broadcasted_iota(jnp.int32, (entries, entries), 1)

    def ones(mask):
        return jnp.where(mask, 1.0, 0.0)

    for source in range(line):

        def spread(e, carry):
            down, across = carry
            slot = asked_ref[e // capacity, 0, source * capacity + e % capacity]
            return jnp.where(row == e, slot, down), jnp.where(column == e, slot, across)

        zero = jnp.zeros((entries, entries), jnp.int32)
        mine, other = lax.fori_loop(0, entries, spread, (zero, zero))
        twin = (other == mine) & (column < row)
        place = jnp.sum(ones((other < mine) | twin), axis=1, keepdims=True)
        shared = jnp.max(ones(twin), axis=1, keepdims=True)
        at = place == column.astype(jnp.float32)
        tables_ref[source, 0:1, :] = jnp.sum(jnp.where(at, row.astype(jnp.float32), 0.0), axis=0, keepdims=True).astype(jnp.int32)
        tables_ref[source, 1:2, :] = jnp.sum(jnp.where(at, shared, 0.0), axis=0, keepdims=True).astype(jnp.int32)
        upto = jnp.sum(ones(mine <= column), axis=0, keepdims=True)
        tables_ref[source, 2:3, :] = jnp.maximum(upto - 1.0, 0.0).astype(jnp.int32)
        tables_ref[source, 3:4, :] = jnp.max(ones(mine == column), axis=0, keepdims=True).astype(jnp.int32)
        tables_ref[source, 4:8, :] = jnp.zeros((4, entries), jnp.int32)


def give_back(
    z, q, plane, line, arrange, tables_ref, stage, prev_ref, out_ref, received, part, running, inbox,
    hop_send, hop_recv, local_sem, send_sem, recv_sem
):
    capacity, width = stage.shape[2:4]
    stored = prev_ref.shape[0]
    entries = plane * capacity
    order = [jnp.where(z == 0, line - 1 - p, jnp.where(z == line - 1, (p + 1) % line, (2, 1, 3, 0)[p])) for p in range(line)]

    def to_mate(p, k):
        to = lax.rem(q + k, plane)
        return pltpu.make_async_remote_copy(
            src_ref=stage.at[lax.rem(z + order[p], line), to],
            dst_ref=received[p].at[pl.ds(q * capacity, capacity)],
            send_sem=send_sem.at[p, k],
            recv_sem=recv_sem.at[p, k],
            device_id=mate(z, to, plane),
            device_id_type=pl.DeviceIdType.MESH,
        )

    def to_self(p):
        return pltpu.make_async_copy(
            stage.at[lax.rem(z + order[p], line), q],
            received[p].at[pl.ds(q * capacity, capacity)],
            local_sem.at[p],
        )

    def exchange(p):
        arrange(lax.rem(z + order[p], line))

        def one(k, carry):
            to_mate(p, k).start()
            return carry

        lax.fori_loop(1, plane, one, 0)
        to_self(p).start()

    def hop(p, up):
        to = order[p] - 1 if up else order[p] + 1
        return pltpu.make_async_remote_copy(
            src_ref=part[p],
            dst_ref=inbox.at[to],
            send_sem=hop_send.at[p],
            recv_sem=hop_recv.at[to],
            device_id=mate(z + 1 if up else z - 1, q, plane),
            device_id_type=pl.DeviceIdType.MESH,
        )

    def arrival(slot):
        return pltpu.make_async_remote_copy(
            src_ref=part[0],
            dst_ref=inbox.at[slot],
            send_sem=hop_send.at[0],
            recv_sem=hop_recv.at[slot],
            device_id=mate(z, lax.rem(q + 1, plane), plane),
            device_id_type=pl.DeviceIdType.MESH,
        )

    def gather(p):
        def finish(k, carry):
            to_mate(p, k).wait()
            return carry

        lax.fori_loop(1, plane, finish, 0)
        to_self(p).wait()
        if p + 2 < line:
            exchange(p + 2)
        row = lax.rem(z + order[p], line)

        def one(k, total):
            tile = received[p][jnp.clip(tables_ref[row, 0, k], 0, entries - 1)].astype(jnp.float32)
            total = jnp.where(tables_ref[row, 1, k] != 0, total, 0.0) + tile
            running[k] = total
            return total

        lax.fori_loop(0, entries, one, jnp.zeros((width, width), jnp.float32), unroll=4)

    def slot_sum(p, t):
        row = lax.rem(z + order[p], line)
        return jnp.where(tables_ref[row, 3, t] != 0, running[jnp.clip(tables_ref[row, 2, t], 0, entries - 1)], 0.0)

    def each(body):
        def one(t, carry):
            body(t)
            return carry

        lax.fori_loop(0, stored, one, 0, unroll=4)

    exchange(0)
    exchange(1)
    for p in range(line - 1):
        gather(p)
        up = z + order[p] < line
        feeds = jnp.where(up, z > 0, z < line - 1)

        @pl.when(feeds)
        def _():
            arrival(order[p]).wait_recv()

            def body(t):
                part[p][t] = (slot_sum(p, t) + inbox[order[p], t].astype(jnp.float32)).astype(jnp.bfloat16)

            each(body)

        @pl.when(jnp.logical_not(feeds))
        def _():
            def body(t):
                part[p][t] = slot_sum(p, t).astype(jnp.bfloat16)

            each(body)

        pl.when(up)(lambda: hop(p, True).start())
        pl.when(jnp.logical_not(up))(lambda: hop(p, False).start())
    gather(line - 1)

    for slot, there in ((0, z > 0), (line, z < line - 1)):

        @pl.when(there)
        def _():
            arrival(slot).wait_recv()

        @pl.when(jnp.logical_not(there))
        def _():
            inbox[slot] = jnp.zeros(inbox.shape[1:], inbox.dtype)

    def last(t):
        total = slot_sum(line - 1, t) + inbox[0, t].astype(jnp.float32) + inbox[line, t].astype(jnp.float32)
        out_ref[t] = prev_ref[t].astype(jnp.float32) - 0.5 * total

    each(last)
    for p in range(line - 1):
        arrival_of = pltpu.make_async_remote_copy(
            src_ref=part[p],
            dst_ref=inbox.at[0],
            send_sem=hop_send.at[p],
            recv_sem=hop_recv.at[0],
            device_id=mate(z, lax.rem(q + 1, plane), plane),
            device_id_type=pl.DeviceIdType.MESH,
        )
        arrival_of.wait_send()


def exchange_kernel(
    plane, line, wanted_ref, scales_ref, pos_ref, inverse_ref, counts_ref, dens_ref, colloc_hbm, coords_ref,
    weights_ref, prev_ref, out_ref, *scratch
):
    pools, received, rest = scratch[:line], scratch[line : 2 * line], scratch[2 * line :]
    stage, fetched_ref, dmat_ref, colloc_ref, metric_ref, asked_vmem, asked_ref, tables_vmem, tables_ref = rest[:9]
    running, inbox, parts_ref = rest[9:12]
    in_sem, smem_sem, ask_send, ask_recv, hop_send, hop_recv, local_sem, send_sem, recv_sem = rest[12:21]
    return_sems = rest[21:]
    capacity, width = stage.shape[2:4]
    listed = colloc_hbm.shape[2] // width
    stored = dens_ref.shape[0]
    batches = colloc_hbm.shape[0]
    me = lax.axis_index("grid")
    z, q = me // plane, lax.rem(me, plane)

    def load(b):
        return pltpu.make_async_copy(colloc_hbm.at[b], colloc_ref.at[lax.rem(b, 2)], in_sem.at[lax.rem(b, 2)])

    load(0).start()

    def scale(t, carry):
        pools[0][t] = (dens_ref[t].astype(jnp.float32) * scales_ref[t]).astype(jnp.bfloat16)
        return carry

    lax.fori_loop(0, stored, scale, 0)
    greet(z, q, plane, line)

    def hop(slot, up):
        to_slot = (slot + 1 if up else slot - 1) % line
        return pltpu.make_async_remote_copy(
            src_ref=pools[slot],
            dst_ref=pools[to_slot],
            send_sem=hop_send.at[line if (slot == 0 and not up) else slot],
            recv_sem=hop_recv.at[to_slot],
            device_id=mate(z + 1 if up else z - 1, q, plane),
            device_id_type=pl.DeviceIdType.MESH,
        )

    def hops(slot, act):
        if slot + 1 < line:

            @pl.when((z >= slot) & (z < line - 1))
            def _():
                act(hop(slot, True))

        if slot != 1:

            @pl.when(((z < slot) | (slot == 0)) & (z > 0))
            def _():
                act(hop(slot, False))

    def to_mate(slot, k):
        owner = lax.rem(z - slot + line, line) * plane + q
        return pltpu.make_async_remote_copy(
            src_ref=stage.at[slot, k],
            dst_ref=fetched_ref.at[pl.ds(owner * capacity, capacity)],
            send_sem=send_sem.at[slot, k],
            recv_sem=recv_sem.at[slot, k],
            device_id=mate(z, lax.rem(q + k, plane), plane),
            device_id_type=pl.DeviceIdType.MESH,
        )

    def to_self(slot):
        owner = lax.rem(z - slot + line, line) * plane + q
        return pltpu.make_async_copy(
            stage.at[slot, 0], fetched_ref.at[pl.ds(owner * capacity, capacity)], local_sem.at[slot]
        )

    def serve(slot):
        if slot:
            hop(slot - 1, True).wait_recv()
            hops(slot, lambda copy: copy.start())
        source = lax.rem(z - slot + line, line)

        def fill(k):
            to = lax.rem(q + k, plane)
            for r in range(capacity):
                stage[slot, k, r] = pools[slot][asked_ref[to, 0, source * capacity + r]]

        def one(k, carry):
            fill(k)
            to_mate(slot, k).start()
            return carry

        lax.fori_loop(1, plane, one, 0)
        fill(0)
        to_self(slot).start()

    def metrics(first, last):
        def one(b, carry):
            load(b).wait()

            @pl.when(b + 1 < batches)
            def _():
                load(b + 1).start()

            metric_kernel(colloc_ref.at[lax.rem(b, 2)], coords_ref.at[b], weights_ref.at[pl.ds(b, 1)], metric_ref.at[b])
            return carry

        lax.fori_loop(first, last, one, 0)

    def ask(k):
        return pltpu.make_async_remote_copy(
            src_ref=wanted_ref.at[lax.rem(q + k, plane)],
            dst_ref=asked_vmem.at[q],
            send_sem=ask_send.at[k],
            recv_sem=ask_recv.at[k],
            device_id=mate(z, lax.rem(q + k, plane), plane),
            device_id_type=pl.DeviceIdType.MESH,
        )

    for k in range(1, plane):
        ask(k).start()
    own = pltpu.make_async_copy(wanted_ref.at[q], asked_vmem.at[q], ask_send.at[0])
    own.start()
    hops(0, lambda copy: copy.start())
    own.wait()
    for k in range(1, plane):
        ask(k).wait()
    scalars = pltpu.make_async_copy(asked_vmem, asked_ref, smem_sem)
    scalars.start()
    scalars.wait()
    serve(0)
    slot_tables(asked_ref, tables_vmem, line, capacity)
    scalars = pltpu.make_async_copy(tables_vmem, tables_ref, smem_sem)
    scalars.start()
    scalars.wait()
    for d in range(1, line):
        metrics(batches * (d - 1) // (line - 1), batches * d // (line - 1))
        if 2 * d == line:
            serve(d)
        else:
            pl.when(z >= d)(functools.partial(serve, d))
            pl.when(z + d < line)(functools.partial(serve, line - d))
    for slot in range(line):
        hops(slot, lambda copy: copy.wait_send())
        to_self(slot).wait()

        def finish(k, carry):
            to_mate(slot, k).wait()
            return carry

        lax.fori_loop(1, plane, finish, 0)

    def product(b, buffer):
        count = counts_ref[b]
        for i in range(listed):
            for j in range(listed):
                tile = fetched_ref[pos_ref[(b * listed + i) * listed + j]]
                dmat_ref[buffer, i * width : (i + 1) * width, j * width : (j + 1) * width] = jnp.where(
                    max(i, j) < count, tile, jnp.zeros_like(tile)
                )
        parts = jnp.dot(metric_ref[b], dmat_ref[buffer], preferred_element_type=jnp.float32)
        for i in range(listed):
            for j in range(listed):
                part = parts[i * width : (i + 1) * width, j * width : (j + 1) * width].astype(jnp.bfloat16)
                parts_ref[(b * listed + i) * listed + j] = jnp.where(max(i, j) < count, part, jnp.zeros_like(part))

    buffers = dmat_ref.shape[0]

    def products(step, carry):
        for buffer in range(buffers):
            product(step * buffers + buffer, buffer)
        return carry

    lax.fori_loop(0, batches // buffers, products, 0)

    def arrange(source):
        def one(lane, carry):
            for r in range(capacity):
                stage[source, lane, r] = parts_ref[inverse_ref[(source * plane + lane) * capacity + r]]
            return carry

        lax.fori_loop(0, plane, one, 0)

    give_back(
        z, q, plane, line, arrange, tables_ref, stage, prev_ref, out_ref, received, pools[1:], running, inbox, *return_sems
    )


def exchange(
    wanted, scales, pos, inverse, counts, dens, collocation, coords, weights, prev, plane, line, capacity
):
    stored, width, _ = dens.shape
    per_dev, points, funcs = collocation.shape
    vmem, smem = pl.BlockSpec(memory_space=pltpu.VMEM), pl.BlockSpec(memory_space=pltpu.SMEM)
    hbm = pl.BlockSpec(memory_space=pl.ANY)
    return pl.pallas_call(
        functools.partial(exchange_kernel, plane, line),
        out_shape=jax.ShapeDtypeStruct(prev.shape, jnp.float32),
        in_specs=[vmem, smem, smem, smem, smem, vmem, hbm, vmem, vmem, vmem],
        out_specs=vmem,
        scratch_shapes=[pltpu.VMEM((stored, width, width), jnp.bfloat16)] * line
        + [pltpu.VMEM((plane * capacity, width, width), jnp.bfloat16)] * line
        + [
            pltpu.VMEM((line, plane, capacity, width, width), jnp.bfloat16),
            pltpu.VMEM((line * plane * capacity, width, width), jnp.bfloat16),
            pltpu.VMEM((2 - per_dev % 2, funcs, funcs), jnp.bfloat16),
            pltpu.VMEM((2, points, funcs), jnp.bfloat16),
            pltpu.VMEM((per_dev, funcs, funcs), jnp.bfloat16),
            pltpu.VMEM(wanted.shape, jnp.int32),
            pltpu.SMEM(wanted.shape, jnp.int32),
            pltpu.VMEM((line, 8, plane * capacity), jnp.int32),
            pltpu.SMEM((line, 8, plane * capacity), jnp.int32),
            pltpu.VMEM((plane * capacity, width, width), jnp.float32),
            pltpu.VMEM((line + 1, stored, width, width), jnp.bfloat16),
            pltpu.VMEM((line * plane * capacity, width, width), jnp.bfloat16),
            pltpu.SemaphoreType.DMA((2,)),
            pltpu.SemaphoreType.DMA,
            pltpu.SemaphoreType.DMA((plane,)),
            pltpu.SemaphoreType.DMA((plane,)),
            pltpu.SemaphoreType.DMA((line + 1,)),
            pltpu.SemaphoreType.DMA((line,)),
            pltpu.SemaphoreType.DMA((line,)),
            pltpu.SemaphoreType.DMA((line, plane)),
            pltpu.SemaphoreType.DMA((line, plane)),
            pltpu.SemaphoreType.DMA((line - 1,)),
            pltpu.SemaphoreType.DMA((line + 1,)),
            pltpu.SemaphoreType.DMA((line,)),
            pltpu.SemaphoreType.DMA((line, plane)),
            pltpu.SemaphoreType.DMA((line, plane)),
        ],
        compiler_params=pltpu.CompilerParams(
            collective_id=0, has_side_effects=True, vmem_limit_bytes=VMEM_BYTES
        ),
        name="exchange",
    )(wanted, scales, pos, inverse, counts, dens, collocation, coords, weights, prev)


def shards(collocation, coords, weights, owners, slots, counts, dens_tiles, dens_scales, fock_prev):
    npeer = lax.axis_size("grid")
    per_dev, npair = owners.shape
    width = dens_tiles.shape[1]
    entries = per_dev * npair
    capacity = entries // npeer
    flat_owner = owners.reshape(-1)
    flat_slot = slots.reshape(-1)
    onehot = (flat_owner[:, None] == jnp.arange(npeer, dtype=jnp.int32)[None, :]).astype(jnp.bfloat16)
    before = jnp.tril(jnp.ones((entries, entries), jnp.bfloat16), -1)
    running = jnp.dot(before, onehot, preferred_element_type=jnp.float32)
    rank = jnp.sum(running * onehot.astype(jnp.float32), axis=1).astype(jnp.int32)
    pos = flat_owner * capacity + rank
    ranked = jnp.where(
        rank[:, None] == jnp.arange(capacity, dtype=jnp.int32)[None, :], flat_slot[:, None], 0
    )
    requests = jnp.dot(
        onehot.T, ranked.astype(jnp.bfloat16), preferred_element_type=jnp.float32
    ).astype(jnp.int32)
    plane = 8
    line = npeer // plane
    if line == 4 and plane * capacity >= dens_tiles.shape[0]:
        wanted = requests.reshape(line, plane, capacity).transpose(1, 0, 2).reshape(plane, 1, line * capacity)
        wanted = jnp.pad(wanted, ((0, 0), (0, 7), (0, 128 - line * capacity)))
        index = jnp.arange(entries, dtype=jnp.int32)[:, None]
        numbered = jnp.where(rank[:, None] == jnp.arange(capacity, dtype=jnp.int32)[None, :], index, 0)
        inverse = jnp.dot(
            onehot.T.astype(jnp.float32), numbered.astype(jnp.float32), precision=lax.Precision.HIGHEST
        ).astype(jnp.int32)
        return exchange(
            wanted, dens_scales, pos, inverse.reshape(-1), counts, dens_tiles, collocation, coords, weights,
            fock_prev, plane, line, capacity,
        )
    asked = lax.all_to_all(requests, "grid", split_axis=0, concat_axis=0, tiled=True).reshape(-1)
    chunk = 16
    tiles = pick(asked, dens_scales, dens_tiles, chunk)
    metric = metric_of(collocation, coords, weights)
    fetched = lax.all_to_all(
        tiles.reshape(npeer, capacity, width, width), "grid", split_axis=0, concat_axis=0, tiled=True
    ).reshape(entries, width, width)
    outgoing = apply_metric(pos, counts, fetched, metric)
    received = lax.all_to_all(
        outgoing.reshape(npeer, capacity, width, width), "grid", split_axis=0, concat_axis=0, tiled=True
    ).reshape(entries, width, width)
    return update(asked, received, fock_prev, chunk)


def solution(mesh):
    split = ("groups", "grid")
    return jax.shard_map(
        shards,
        mesh=mesh,
        in_specs=(
            P(split, None, None),
            P(split, None, None),
            P(split, None),
            P(split, None),
            P(split, None),
            P(split),
            P(split, None, None),
            P(split),
            P(split, None, None),
        ),
        out_specs=P(split, None, None),
        check_vma=False,
    )
```

```python
import functools

import jax
import jax.numpy as jnp
from jax import lax
from jax.experimental import pallas as pl
from jax.experimental.pallas import tpu as pltpu
from jax.sharding import PartitionSpec as P

SOFTEN = 0.5
VMEM_BYTES = 62 * 2**20


def metric_kernel(colloc_ref, coords_ref, weights_ref, metric_ref):
    points = colloc_ref.shape[0]
    xyz = coords_ref[...]
    w = weights_ref[...]
    rows = jnp.concatenate([xyz, w, jnp.zeros((4, points), jnp.float32)], axis=0)
    cols = rows.T
    a = colloc_ref[...]
    total = jnp.full((points, points), SOFTEN * SOFTEN, jnp.float32)
    for axis in range(3):
        diff = cols[:, axis : axis + 1] - xyz[axis : axis + 1, :]
        total = total + diff * diff
    kern = (cols[:, 3:4] * w * lax.rsqrt(total)).astype(jnp.bfloat16)
    smeared = jnp.dot(kern, a, preferred_element_type=jnp.float32).astype(jnp.bfloat16)
    metric_ref[...] = lax.dot_general(
        a, smeared, (((0,), (0,)), ((), ())), preferred_element_type=jnp.float32
    ).astype(jnp.bfloat16)


def metric_of(collocation, coords, weights):
    per_dev, points, funcs = collocation.shape
    return pl.pallas_call(
        metric_kernel,
        grid=(per_dev,),
        out_shape=jax.ShapeDtypeStruct((per_dev, funcs, funcs), jnp.bfloat16),
        in_specs=[
            pl.BlockSpec((None, points, funcs), lambda b: (b, 0, 0)),
            pl.BlockSpec((None, 3, points), lambda b: (b, 0, 0)),
            pl.BlockSpec((None, 1, points), lambda b: (b, 0, 0)),
        ],
        out_specs=pl.BlockSpec((None, funcs, funcs), lambda b: (b, 0, 0)),
        compiler_params=pltpu.CompilerParams(vmem_limit_bytes=VMEM_BYTES),
        cost_estimate=pl.CostEstimate(
            flops=4 * per_dev * points * points * funcs,
            bytes_accessed=4 * per_dev * points * funcs,
            transcendentals=per_dev * points * points,
        ),
        name="metric",
    )(collocation, coords, weights[:, None, :])


def pick_kernel(asked_ref, scales_ref, dens_ref, out_ref, scaled):
    stored = dens_ref.shape[0]
    count = out_ref.shape[0]
    step = pl.program_id(0)

    @pl.when(step == 0)
    def _():
        def one(t, carry):
            scaled[t] = (dens_ref[t].astype(jnp.float32) * scales_ref[t]).astype(jnp.bfloat16)
            return carry

        lax.fori_loop(0, stored, one, 0)

    for k in range(count):
        out_ref[k] = scaled[asked_ref[step * count + k]]


def pick(asked, scales, dens, chunk):
    total = asked.shape[0]
    stored, width, _ = dens.shape
    return pl.pallas_call(
        pick_kernel,
        out_shape=jax.ShapeDtypeStruct((total, width, width), jnp.bfloat16),
        grid_spec=pltpu.PrefetchScalarGridSpec(
            num_scalar_prefetch=2,
            grid=(total // chunk,),
            in_specs=[pl.BlockSpec((stored, width, width), lambda s, *_: (0, 0, 0))],
            out_specs=pl.BlockSpec((chunk, width, width), lambda s, *_: (s, 0, 0)),
            scratch_shapes=[pltpu.VMEM((stored, width, width), jnp.bfloat16)],
        ),
        compiler_params=pltpu.CompilerParams(vmem_limit_bytes=VMEM_BYTES),
        name="pick",
    )(asked, scales, dens)


def apply_kernel(listed, pos_ref, counts_ref, fetched_ref, metric_ref, out_ref, dmat):
    width = fetched_ref.shape[1]
    b = pl.program_id(0)
    count = jnp.clip(counts_ref[b], 0, listed)

    def at(i, j):
        return pos_ref[b * listed * listed + i * listed + j]

    def live(size):
        for i in range(size):
            for j in range(size):
                dmat[i * width : (i + 1) * width, j * width : (j + 1) * width] = fetched_ref[at(i, j)]
        span = size * width
        for i in range(size):
            parts = jnp.dot(
                metric_ref[i * width : (i + 1) * width, :span], dmat[:span, :span], preferred_element_type=jnp.float32
            ).astype(jnp.bfloat16)
            for j in range(size):
                out_ref[at(i, j)] = parts[:, j * width : (j + 1) * width]

    def branch(size):
        if size:
            live(size)
        for i in range(listed):
            for j in range(listed):
                if max(i, j) >= size:
                    out_ref[at(i, j)] = jnp.zeros((width, width), jnp.bfloat16)

    for size in range(listed + 1):
        pl.when(count == size)(functools.partial(branch, size))


def apply_metric(pos, counts, fetched, metric):
    total, width, _ = fetched.shape
    per_dev, funcs, _ = metric.shape
    return pl.pallas_call(
        functools.partial(apply_kernel, funcs // width),
        out_shape=jax.ShapeDtypeStruct((total, width, width), jnp.bfloat16),
        grid_spec=pltpu.PrefetchScalarGridSpec(
            num_scalar_prefetch=2,
            grid=(per_dev,),
            in_specs=[
                pl.BlockSpec(
                    (total, width, width), lambda b, *_: (0, 0, 0), pipeline_mode=pl.Buffered(1)
                ),
                pl.BlockSpec((None, funcs, funcs), lambda b, *_: (b, 0, 0)),
            ],
            out_specs=pl.BlockSpec((total, width, width), lambda b, *_: (0, 0, 0)),
            scratch_shapes=[pltpu.VMEM((funcs, funcs), jnp.bfloat16)],
        ),
        compiler_params=pltpu.CompilerParams(vmem_limit_bytes=VMEM_BYTES),
        name="apply_metric",
    )(pos, counts, fetched, metric)


def update_kernel(asked_ref, received_ref, prev_ref, out_ref):
    count = received_ref.shape[0]
    step = pl.program_id(0)

    @pl.when(step == 0)
    def _():
        out_ref[...] = prev_ref[...].astype(jnp.float32)

    for k in range(count):
        slot = asked_ref[step * count + k]
        out_ref[slot] = out_ref[slot] - 0.5 * received_ref[k].astype(jnp.float32)


def update(asked, received, prev, chunk):
    total, width, _ = received.shape
    stored = prev.shape[0]
    return pl.pallas_call(
        update_kernel,
        out_shape=jax.ShapeDtypeStruct((stored, width, width), jnp.float32),
        grid_spec=pltpu.PrefetchScalarGridSpec(
            num_scalar_prefetch=1,
            grid=(total // chunk,),
            in_specs=[
                pl.BlockSpec((chunk, width, width), lambda s, *_: (s, 0, 0)),
                pl.BlockSpec((stored, width, width), lambda s, *_: (0, 0, 0)),
            ],
            out_specs=pl.BlockSpec((stored, width, width), lambda s, *_: (0, 0, 0)),
        ),
        compiler_params=pltpu.CompilerParams(vmem_limit_bytes=VMEM_BYTES),
        name="update",
    )(asked, received, prev)


def mate(z, lane, plane):
    return {"grid": z * plane + lane}


def greet(z, q, plane, line):
    barrier = pltpu.get_barrier_semaphore()
    for k in range(1, plane):
        pl.semaphore_signal(
            barrier, inc=1, device_id=mate(z, lax.rem(q + k, plane), plane), device_id_type=pl.DeviceIdType.MESH
        )

    @pl.when(z > 0)
    def _():
        pl.semaphore_signal(barrier, inc=1, device_id=mate(z - 1, q, plane), device_id_type=pl.DeviceIdType.MESH)

    @pl.when(z < line - 1)
    def _():
        pl.semaphore_signal(barrier, inc=1, device_id=mate(z + 1, q, plane), device_id_type=pl.DeviceIdType.MESH)

    pl.semaphore_wait(barrier, plane - 1 + jnp.where(z > 0, 1, 0) + jnp.where(z < line - 1, 1, 0))


def slot_tables(asked_ref, tables_ref, line, capacity):
    entries = tables_ref.shape[2]
    row = lax.broadcasted_iota(jnp.int32, (entries, entries), 0)
    column = lax.broadcasted_iota(jnp.int32, (entries, entries), 1)

    def ones(mask):
        return jnp.where(mask, 1.0, 0.0)

    for source in range(line):

        def spread(e, carry):
            down, across = carry
            slot = asked_ref[e // capacity, 0, source * capacity + e % capacity]
            return jnp.where(row == e, slot, down), jnp.where(column == e, slot, across)

        zero = jnp.zeros((entries, entries), jnp.int32)
        mine, other = lax.fori_loop(0, entries, spread, (zero, zero))
        twin = (other == mine) & (column < row)
        place = jnp.sum(ones((other < mine) | twin), axis=1, keepdims=True)
        shared = jnp.max(ones(twin), axis=1, keepdims=True)
        at = place == column.astype(jnp.float32)
        tables_ref[source, 0:1, :] = jnp.sum(jnp.where(at, row.astype(jnp.float32), 0.0), axis=0, keepdims=True).astype(jnp.int32)
        tables_ref[source, 1:2, :] = jnp.sum(jnp.where(at, shared, 0.0), axis=0, keepdims=True).astype(jnp.int32)
        upto = jnp.sum(ones(mine <= column), axis=0, keepdims=True)
        tables_ref[source, 2:3, :] = jnp.maximum(upto - 1.0, 0.0).astype(jnp.int32)
        tables_ref[source, 3:4, :] = jnp.max(ones(mine == column), axis=0, keepdims=True).astype(jnp.int32)
        tables_ref[source, 4:8, :] = jnp.zeros((4, entries), jnp.int32)


def give_back(
    z, q, plane, line, arrange, tables_ref, stage, prev_ref, out_ref, received, part, running, inbox,
    hop_send, hop_recv, local_sem, send_sem, recv_sem, out_hbm, out_sem
):
    capacity, width = stage.shape[2:4]
    stored = prev_ref.shape[0]
    entries = plane * capacity
    order = [jnp.where(z == 0, line - 1 - p, jnp.where(z == line - 1, (p + 1) % line, (2, 1, 3, 0)[p])) for p in range(line)]

    def to_mate(p, k):
        to = lax.rem(q + k, plane)
        return pltpu.make_async_remote_copy(
            src_ref=stage.at[lax.rem(z + order[p], line), to],
            dst_ref=received[p].at[pl.ds(q * capacity, capacity)],
            send_sem=send_sem.at[p, k],
            recv_sem=recv_sem.at[p, k],
            device_id=mate(z, to, plane),
            device_id_type=pl.DeviceIdType.MESH,
        )

    def to_self(p):
        return pltpu.make_async_copy(
            stage.at[lax.rem(z + order[p], line), q],
            received[p].at[pl.ds(q * capacity, capacity)],
            local_sem.at[p],
        )

    def exchange(p):
        arrange(lax.rem(z + order[p], line))

        def one(k, carry):
            to_mate(p, k).start()
            return carry

        lax.fori_loop(1, plane, one, 0)
        to_self(p).start()

    def hop(p, up):
        to = order[p] - 1 if up else order[p] + 1
        return pltpu.make_async_remote_copy(
            src_ref=part[p],
            dst_ref=inbox.at[to],
            send_sem=hop_send.at[p],
            recv_sem=hop_recv.at[to],
            device_id=mate(z + 1 if up else z - 1, q, plane),
            device_id_type=pl.DeviceIdType.MESH,
        )

    def arrival(slot):
        return pltpu.make_async_remote_copy(
            src_ref=part[0],
            dst_ref=inbox.at[slot],
            send_sem=hop_send.at[0],
            recv_sem=hop_recv.at[slot],
            device_id=mate(z, lax.rem(q + 1, plane), plane),
            device_id_type=pl.DeviceIdType.MESH,
        )

    def gather(p):
        def finish(k, carry):
            to_mate(p, k).wait()
            return carry

        lax.fori_loop(1, plane, finish, 0)
        to_self(p).wait()
        if p + 2 < line:
            exchange(p + 2)
        row = lax.rem(z + order[p], line)

        def one(k, total):
            tile = received[p][jnp.clip(tables_ref[row, 0, k], 0, entries - 1)].astype(jnp.float32)
            total = jnp.where(tables_ref[row, 1, k] != 0, total, 0.0) + tile
            running[k] = total
            return total

        lax.fori_loop(0, entries, one, jnp.zeros((width, width), jnp.float32), unroll=4)

    def slot_sum(p, t):
        row = lax.rem(z + order[p], line)
        return jnp.where(tables_ref[row, 3, t] != 0, running[jnp.clip(tables_ref[row, 2, t], 0, entries - 1)], 0.0)

    def each(body):
        def one(t, carry):
            body(t)
            return carry

        lax.fori_loop(0, stored, one, 0, unroll=4)

    exchange(0)
    exchange(1)
    for p in range(line - 1):
        gather(p)
        up = z + order[p] < line
        feeds = jnp.where(up, z > 0, z < line - 1)

        @pl.when(feeds)
        def _():
            arrival(order[p]).wait_recv()

            def body(t):
                part[p][t] = (slot_sum(p, t) + inbox[order[p], t].astype(jnp.float32)).astype(jnp.bfloat16)

            each(body)

        @pl.when(jnp.logical_not(feeds))
        def _():
            def body(t):
                part[p][t] = slot_sum(p, t).astype(jnp.bfloat16)

            each(body)

        pl.when(up)(lambda: hop(p, True).start())
        pl.when(jnp.logical_not(up))(lambda: hop(p, False).start())
    gather(line - 1)

    for slot, there in ((0, z > 0), (line, z < line - 1)):

        @pl.when(there)
        def _():
            arrival(slot).wait_recv()

        @pl.when(jnp.logical_not(there))
        def _():
            inbox[slot] = jnp.zeros(inbox.shape[1:], inbox.dtype)

    def last(t):
        total = slot_sum(line - 1, t) + inbox[0, t].astype(jnp.float32) + inbox[line, t].astype(jnp.float32)
        out_ref[t] = prev_ref[t].astype(jnp.float32) - 0.5 * total

    halves = [pl.ds(h * (stored // 2), stored // 2) for h in range(2)]
    for h, rows in enumerate(halves):

        def some(t, carry):
            last(h * (stored // 2) + t)
            return carry

        lax.fori_loop(0, stored // 2, some, 0, unroll=4)
        pltpu.make_async_copy(out_ref.at[rows], out_hbm.at[rows], out_sem.at[h]).start()
    for h, rows in enumerate(halves):
        pltpu.make_async_copy(out_ref.at[rows], out_hbm.at[rows], out_sem.at[h]).wait()
    for p in range(line - 1):
        arrival_of = pltpu.make_async_remote_copy(
            src_ref=part[p],
            dst_ref=inbox.at[0],
            send_sem=hop_send.at[p],
            recv_sem=hop_recv.at[0],
            device_id=mate(z, lax.rem(q + 1, plane), plane),
            device_id_type=pl.DeviceIdType.MESH,
        )
        arrival_of.wait_send()


def exchange_kernel(
    plane, line, wanted_ref, scales_ref, pos_ref, inverse_ref, counts_ref, dens_ref, colloc_hbm, coords_ref,
    weights_ref, prev_ref, out_hbm, *scratch
):
    pools, received, rest = scratch[:line], scratch[line : 2 * line], scratch[2 * line :]
    stage, fetched_ref, dmat_ref, colloc_ref, metric_ref, asked_vmem, asked_ref, tables_vmem, tables_ref = rest[:9]
    running, inbox, parts_ref, out_ref, out_sem = rest[9:14]
    in_sem, smem_sem, ask_send, ask_recv, hop_send, hop_recv, local_sem, send_sem, recv_sem = rest[14:23]
    return_sems = rest[23:]
    capacity, width = stage.shape[2:4]
    listed = colloc_hbm.shape[2] // width
    stored = dens_ref.shape[0]
    batches = colloc_hbm.shape[0]
    me = lax.axis_index("grid")
    z, q = me // plane, lax.rem(me, plane)

    def load(b):
        return pltpu.make_async_copy(colloc_hbm.at[b], colloc_ref.at[lax.rem(b, 2)], in_sem.at[lax.rem(b, 2)])

    load(0).start()

    def scale(t, carry):
        pools[0][t] = (dens_ref[t].astype(jnp.float32) * scales_ref[t]).astype(jnp.bfloat16)
        return carry

    lax.fori_loop(0, stored, scale, 0)
    greet(z, q, plane, line)

    def hop(slot, up):
        to_slot = (slot + 1 if up else slot - 1) % line
        return pltpu.make_async_remote_copy(
            src_ref=pools[slot],
            dst_ref=pools[to_slot],
            send_sem=hop_send.at[line if (slot == 0 and not up) else slot],
            recv_sem=hop_recv.at[to_slot],
            device_id=mate(z + 1 if up else z - 1, q, plane),
            device_id_type=pl.DeviceIdType.MESH,
        )

    def hops(slot, act):
        if slot + 1 < line:

            @pl.when((z >= slot) & (z < line - 1))
            def _():
                act(hop(slot, True))

        if slot != 1:

            @pl.when(((z < slot) | (slot == 0)) & (z > 0))
            def _():
                act(hop(slot, False))

    def to_mate(slot, k):
        owner = lax.rem(z - slot + line, line) * plane + q
        return pltpu.make_async_remote_copy(
            src_ref=stage.at[slot, k],
            dst_ref=fetched_ref.at[pl.ds(owner * capacity, capacity)],
            send_sem=send_sem.at[slot, k],
            recv_sem=recv_sem.at[slot, k],
            device_id=mate(z, lax.rem(q + k, plane), plane),
            device_id_type=pl.DeviceIdType.MESH,
        )

    def to_self(slot):
        owner = lax.rem(z - slot + line, line) * plane + q
        return pltpu.make_async_copy(
            stage.at[slot, 0], fetched_ref.at[pl.ds(owner * capacity, capacity)], local_sem.at[slot]
        )

    def serve(slot):
        if slot:
            hop(slot - 1, True).wait_recv()
            hops(slot, lambda copy: copy.start())
        source = lax.rem(z - slot + line, line)

        def fill(k):
            to = lax.rem(q + k, plane)
            for r in range(capacity):
                stage[slot, k, r] = pools[slot][asked_ref[to, 0, source * capacity + r]]

        def one(k, carry):
            fill(k)
            to_mate(slot, k).start()
            return carry

        lax.fori_loop(1, plane, one, 0)
        fill(0)
        to_self(slot).start()

    def metrics(first, last):
        def one(b, carry):
            load(b).wait()

            @pl.when(b + 1 < batches)
            def _():
                load(b + 1).start()

            metric_kernel(colloc_ref.at[lax.rem(b, 2)], coords_ref.at[b], weights_ref.at[pl.ds(b, 1)], metric_ref.at[b])
            return carry

        lax.fori_loop(first, last, one, 0)

    def ask(k):
        return pltpu.make_async_remote_copy(
            src_ref=wanted_ref.at[lax.rem(q + k, plane)],
            dst_ref=asked_vmem.at[q],
            send_sem=ask_send.at[k],
            recv_sem=ask_recv.at[k],
            device_id=mate(z, lax.rem(q + k, plane), plane),
            device_id_type=pl.DeviceIdType.MESH,
        )

    for k in range(1, plane):
        ask(k).start()
    own = pltpu.make_async_copy(wanted_ref.at[q], asked_vmem.at[q], ask_send.at[0])
    own.start()
    hops(0, lambda copy: copy.start())
    own.wait()
    for k in range(1, plane):
        ask(k).wait()
    scalars = pltpu.make_async_copy(asked_vmem, asked_ref, smem_sem)
    scalars.start()
    scalars.wait()
    serve(0)
    slot_tables(asked_ref, tables_vmem, line, capacity)
    scalars = pltpu.make_async_copy(tables_vmem, tables_ref, smem_sem)
    scalars.start()
    scalars.wait()
    for d in range(1, line):
        metrics(batches * (d - 1) // (line - 1), batches * d // (line - 1))
        if 2 * d == line:
            serve(d)
        else:
            pl.when(z >= d)(functools.partial(serve, d))
            pl.when(z + d < line)(functools.partial(serve, line - d))
    for slot in range(line):
        hops(slot, lambda copy: copy.wait_send())
        to_self(slot).wait()

        def finish(k, carry):
            to_mate(slot, k).wait()
            return carry

        lax.fori_loop(1, plane, finish, 0)

    def product(b, buffer):
        count = counts_ref[b]
        for i in range(listed):
            for j in range(listed):
                tile = fetched_ref[pos_ref[(b * listed + i) * listed + j]]
                dmat_ref[buffer, i * width : (i + 1) * width, j * width : (j + 1) * width] = jnp.where(
                    max(i, j) < count, tile, jnp.zeros_like(tile)
                )
        parts = jnp.dot(metric_ref[b], dmat_ref[buffer], preferred_element_type=jnp.float32)
        for i in range(listed):
            for j in range(listed):
                part = parts[i * width : (i + 1) * width, j * width : (j + 1) * width].astype(jnp.bfloat16)
                parts_ref[(b * listed + i) * listed + j] = jnp.where(max(i, j) < count, part, jnp.zeros_like(part))

    buffers = dmat_ref.shape[0]

    def products(step, carry):
        for buffer in range(buffers):
            product(step * buffers + buffer, buffer)
        return carry

    lax.fori_loop(0, batches // buffers, products, 0)

    def arrange(source):
        def one(lane, carry):
            for r in range(capacity):
                stage[source, lane, r] = parts_ref[inverse_ref[(source * plane + lane) * capacity + r]]
            return carry

        lax.fori_loop(0, plane, one, 0)

    give_back(
        z, q, plane, line, arrange, tables_ref, stage, prev_ref, out_ref, received, pools[1:], running, inbox, *return_sems,
        out_hbm, out_sem
    )


def exchange(
    wanted, scales, pos, inverse, counts, dens, collocation, coords, weights, prev, plane, line, capacity
):
    stored, width, _ = dens.shape
    per_dev, points, funcs = collocation.shape
    vmem, smem = pl.BlockSpec(memory_space=pltpu.VMEM), pl.BlockSpec(memory_space=pltpu.SMEM)
    hbm = pl.BlockSpec(memory_space=pl.ANY)
    return pl.pallas_call(
        functools.partial(exchange_kernel, plane, line),
        out_shape=jax.ShapeDtypeStruct(prev.shape, jnp.float32),
        in_specs=[vmem, smem, smem, smem, smem, vmem, hbm, vmem, vmem, vmem],
        out_specs=hbm,
        scratch_shapes=[pltpu.VMEM((stored, width, width), jnp.bfloat16)] * line
        + [pltpu.VMEM((plane * capacity, width, width), jnp.bfloat16)] * line
        + [
            pltpu.VMEM((line, plane, capacity, width, width), jnp.bfloat16),
            pltpu.VMEM((line * plane * capacity, width, width), jnp.bfloat16),
            pltpu.VMEM((2 - per_dev % 2, funcs, funcs), jnp.bfloat16),
            pltpu.VMEM((2, points, funcs), jnp.bfloat16),
            pltpu.VMEM((per_dev, funcs, funcs), jnp.bfloat16),
            pltpu.VMEM(wanted.shape, jnp.int32),
            pltpu.SMEM(wanted.shape, jnp.int32),
            pltpu.VMEM((line, 8, plane * capacity), jnp.int32),
            pltpu.SMEM((line, 8, plane * capacity), jnp.int32),
            pltpu.VMEM((plane * capacity, width, width), jnp.float32),
            pltpu.VMEM((line + 1, stored, width, width), jnp.bfloat16),
            pltpu.VMEM((line * plane * capacity, width, width), jnp.bfloat16),
            pltpu.VMEM((stored, width, width), jnp.float32),
            pltpu.SemaphoreType.DMA((2,)),
            pltpu.SemaphoreType.DMA((2,)),
            pltpu.SemaphoreType.DMA,
            pltpu.SemaphoreType.DMA((plane,)),
            pltpu.SemaphoreType.DMA((plane,)),
            pltpu.SemaphoreType.DMA((line + 1,)),
            pltpu.SemaphoreType.DMA((line,)),
            pltpu.SemaphoreType.DMA((line,)),
            pltpu.SemaphoreType.DMA((line, plane)),
            pltpu.SemaphoreType.DMA((line, plane)),
            pltpu.SemaphoreType.DMA((line - 1,)),
            pltpu.SemaphoreType.DMA((line + 1,)),
            pltpu.SemaphoreType.DMA((line,)),
            pltpu.SemaphoreType.DMA((line, plane)),
            pltpu.SemaphoreType.DMA((line, plane)),
        ],
        compiler_params=pltpu.CompilerParams(
            collective_id=0, has_side_effects=True, vmem_limit_bytes=VMEM_BYTES
        ),
        name="exchange",
    )(wanted, scales, pos, inverse, counts, dens, collocation, coords, weights, prev)


def shards(collocation, coords, weights, owners, slots, counts, dens_tiles, dens_scales, fock_prev):
    npeer = lax.axis_size("grid")
    per_dev, npair = owners.shape
    width = dens_tiles.shape[1]
    entries = per_dev * npair
    capacity = entries // npeer
    flat_owner = owners.reshape(-1)
    flat_slot = slots.reshape(-1)
    onehot = (flat_owner[:, None] == jnp.arange(npeer, dtype=jnp.int32)[None, :]).astype(jnp.bfloat16)
    batch = jnp.arange(per_dev, dtype=jnp.int32)
    named = jnp.sum(onehot.reshape(per_dev, npair, npeer).astype(jnp.float32), axis=1)
    running = jnp.sum(jnp.where((batch[None, :] < batch[:, None])[:, :, None], named[None], 0.0), axis=1)
    rank = jnp.sum(onehot.reshape(per_dev, npair, npeer) * running[:, None, :], axis=2).reshape(-1).astype(jnp.int32)
    pos = flat_owner * capacity + rank
    ranked = jnp.where(
        rank[:, None] == jnp.arange(capacity, dtype=jnp.int32)[None, :], flat_slot[:, None], 0
    )
    requests = jnp.dot(
        onehot.T, ranked.astype(jnp.bfloat16), preferred_element_type=jnp.float32
    ).astype(jnp.int32)
    plane = 8
    line = npeer // plane
    if line == 4 and plane * capacity >= dens_tiles.shape[0]:
        wanted = requests.reshape(line, plane, capacity).transpose(1, 0, 2).reshape(plane, 1, line * capacity)
        wanted = jnp.pad(wanted, ((0, 0), (0, 7), (0, 128 - line * capacity)))
        index = jnp.arange(entries, dtype=jnp.int32)[:, None]
        numbered = jnp.where(rank[:, None] == jnp.arange(capacity, dtype=jnp.int32)[None, :], index, 0)
        inverse = jnp.dot(
            onehot.T.astype(jnp.float32), numbered.astype(jnp.float32), precision=lax.Precision.HIGHEST
        ).astype(jnp.int32)
        return exchange(
            wanted, dens_scales, pos, inverse.reshape(-1), counts, dens_tiles, collocation, coords, weights,
            fock_prev, plane, line, capacity,
        )
    asked = lax.all_to_all(requests, "grid", split_axis=0, concat_axis=0, tiled=True).reshape(-1)
    chunk = 16
    tiles = pick(asked, dens_scales, dens_tiles, chunk)
    metric = metric_of(collocation, coords, weights)
    fetched = lax.all_to_all(
        tiles.reshape(npeer, capacity, width, width), "grid", split_axis=0, concat_axis=0, tiled=True
    ).reshape(entries, width, width)
    outgoing = apply_metric(pos, counts, fetched, metric)
    received = lax.all_to_all(
        outgoing.reshape(npeer, capacity, width, width), "grid", split_axis=0, concat_axis=0, tiled=True
    ).reshape(entries, width, width)
    return update(asked, received, fock_prev, chunk)


def solution(mesh):
    split = ("groups", "grid")
    return jax.shard_map(
        shards,
        mesh=mesh,
        in_specs=(
            P(split, None, None),
            P(split, None, None),
            P(split, None),
            P(split, None),
            P(split, None),
            P(split),
            P(split, None, None),
            P(split),
            P(split, None, None),
        ),
        out_specs=P(split, None, None),
        check_vma=False,
    )
```
